256 devices in a mesh: dp: 4 (over x), fsdp: 4 (over z_hi), row: 16 (over y, z_lo, core).
Axes of the slice: x: 4, y: 4, z: 8 (z_hi: 4, z_lo: 2; z = z_hi * 2 + z_lo), core: 2. Of those that a mesh axis runs over, the one named last changes fastest.
Arguments:
- patches: bfloat16 [16, 32, 128, 2048], P(('dp', 'fsdp'), 'row'), may hold values from -6 to 6
- q_rows: bfloat16 [16, 32, 128, 1024], P(('dp', 'fsdp'), 'row'), may hold values from -4.5 to 4.5
- k_rows: bfloat16 [16, 32, 128, 1024], P(('dp', 'fsdp'), 'row'), may hold values from -4.5 to 4.5
- v_rows: bfloat16 [16, 32, 128, 1024], P(('dp', 'fsdp'), 'row'), may hold values from -6 to 6
- w_out: bfloat16 [1024, 2048], P(('fsdp', 'row')), may hold values from -0.1875 to 0.1875
- gain: bfloat16 [2048], replicated, may hold values from 0.099609375 to 1.8984375
- w_val: bfloat16 [2048, 1024], P(('fsdp', 'row')), may hold values from -0.125 to 0.125
- q_cols: bfloat16 [16, 32, 128, 1024], P(('dp', 'fsdp'), None, 'row'), may hold values from -4.5 to 4.5
- k_cols: bfloat16 [16, 32, 128, 1024], P(('dp', 'fsdp'), None, 'row'), may hold values from -4.5 to 4.5
- cotangent: bfloat16 [16, 32, 128, 1024], P(('dp', 'fsdp'), None, 'row'), may hold values from -6 to 6
Outputs:
- grad_patches: bfloat16 [16, 32, 128, 2048], P(('dp', 'fsdp'), 'row')
- grad_q_rows: bfloat16 [16, 32, 128, 1024], P(('dp', 'fsdp'), 'row')
- grad_k_rows: bfloat16 [16, 32, 128, 1024], P(('dp', 'fsdp'), 'row')
- grad_v_rows: bfloat16 [16, 32, 128, 1024], P(('dp', 'fsdp'), 'row')
- grad_q_cols: bfloat16 [16, 32, 128, 1024], P(('dp', 'fsdp'), None, 'row')
- grad_k_cols: bfloat16 [16, 32, 128, 1024], P(('dp', 'fsdp'), None, 'row')
- grad_w_out: float32 [1024, 2048], P(('fsdp', 'row'))
- grad_w_val: float32 [2048, 1024], P(('fsdp', 'row'))
The draws below stay inside these ranges and needn't reach their ends.
All inputs are finite; a program needn't handle non-finite values.
Results may differ from the reference program's by a relative error of at most 0.014.
Values may be sent and summed in bfloat16 or wider, within the bound.
A program may use at most 192 MiB of HBM per device.

```python
import math
import jax
import jax.numpy as jnp
from jax import lax

D = 2048
HEADS = 8
HD = 128
GW = 128
HW = 1024
H = 32
IMAGES = 16


def planted(key, seq_dim):
    shape = (IMAGES, H, GW, HEADS, HD)
    small = [IMAGES, H, GW, HEADS, 1]
    small[seq_dim] = 1
    sign_shape = list(shape)
    sign_shape[seq_dim] = 1
    base_q = jax.random.normal(jax.random.fold_in(key, 1), shape, jnp.float32)
    base_k = jax.random.normal(jax.random.fold_in(key, 3), shape, jnp.float32)
    base_q = jnp.clip(base_q, -4.5, 4.5)
    base_k = jnp.clip(base_k, -4.5, 4.5)
    position = lax.broadcasted_iota(jnp.int32, shape, seq_dim)
    length = shape[seq_dim]
    queries = jnp.where(position == length - 1, base_q, base_q)
    key_block = jnp.where(position == 0, base_k, base_k)
    key_block = jnp.where(position == 1, base_k, key_block)
    return (queries.reshape(IMAGES, H, GW, HEADS * HD), key_block.reshape(IMAGES, H, GW, HEADS * HD))


def draw_q_rows(key, part):
    both = planted(jax.random.fold_in(key, 100), 2)
    return both[0].astype(jnp.bfloat16)


def draw_k_rows(key, part):
    both = planted(jax.random.fold_in(key, 100), 2)
    return both[1].astype(jnp.bfloat16)


def draw_q_cols(key, part):
    both = planted(jax.random.fold_in(key, 200), 1)
    return both[0].astype(jnp.bfloat16)


def draw_k_cols(key, part):
    both = planted(jax.random.fold_in(key, 200), 1)
    return both[1].astype(jnp.bfloat16)


def strengthened(array, key, source, target, blocks, factor):
    owner, partner = [(jnp.arange(array.shape[axis_at]) // (array.shape[axis_at] // blocks)).reshape([-1 if axis == axis_at else 1 for axis in range(array.ndim)]) for axis_at in (source, target)]
    chosen = jax.random.permutation(key, blocks)[partner]
    strong = (owner == chosen) | (owner == (partner + blocks // 2) % blocks)
    return jnp.where(strong, factor * array, array)


def steps_of(own_key, dims, shards, least, largest):
    factor_of, own = 1.0, jax.random.fold_in(own_key, 6)
    for dim, parts in shards:
        draws = jnp.exp(jax.random.uniform(jax.random.fold_in(own, dim), (parts,), jnp.float32, least / len(shards), largest / len(shards)))
        factor_of = factor_of * jnp.repeat(draws, dims[dim] // parts).reshape([-1 if axis == dim else 1 for axis in range(len(dims))])
    return factor_of


def noise(own_key, extent, scale, most, pieces=(), kind=jnp.bfloat16):
    values = scale * jax.random.normal(own_key, extent, jnp.float32)
    if pieces:
        values = values * steps_of(own_key, extent, pieces, -0.22, 0.18)
    return jnp.clip(values, -most, most).astype(kind)


def bell_draw_with(rng, extent, deviation, most, cuts, heavy, held_as=jnp.bfloat16):
    values = deviation * jax.random.normal(rng, extent, jnp.float32)
    if cuts:
        values = values * steps_of(rng, extent, cuts, -0.22, 0.18)
    return jnp.clip(strengthened(values, jax.random.fold_in(rng, 3), *heavy), -most, most).astype(held_as)


def setup_inputs(seed: int = 0) -> dict:
    streams_of = jax.random.split(jax.random.key(seed), 11)
    patches = bell_draw_with(streams_of[0], (IMAGES, H, GW, D), 1.0, 6.0, ((0, 16), (1, 16)), (1, 3, 16, 2.0))
    q_rows = draw_q_rows(jax.random.fold_in(streams_of[10], 71), 0)
    k_rows = draw_k_rows(jax.random.fold_in(streams_of[10], 71), 0)
    v_rows = bell_draw_with(streams_of[3], (IMAGES, H, GW, HW), 1.0, 6.0, ((0, 16), (1, 16)), (1, 3, 16, 2.0))
    w_out = noise(streams_of[4], (HW, D), HW ** -0.5, 0.1875, ((0, 64),))
    gain = jnp.clip(1.0 + 0.18 * jax.random.normal(streams_of[5], (D,), jnp.float32), 0.099609375, 1.8984375).astype(jnp.bfloat16)
    w_val = noise(streams_of[6], (D, HW), D ** -0.5, 0.125, ((0, 64),))
    q_cols = draw_q_cols(jax.random.fold_in(streams_of[10], 71), 0)
    k_cols = draw_k_cols(jax.random.fold_in(streams_of[10], 71), 0)
    cotangent = noise(streams_of[9], (IMAGES, H, GW, HW), 1.0, 6.0, ((0, 16), (2, 16)))
    return dict(patches=patches, q_rows=q_rows, k_rows=k_rows, v_rows=v_rows, w_out=w_out, gain=gain, w_val=w_val, q_cols=q_cols, k_cols=k_cols, cotangent=cotangent)


def rounded(values):
    return lax.optimization_barrier(values.astype(jnp.bfloat16)).astype(jnp.float32)

def split_heads(values):
    return values.astype(jnp.float32).reshape(values.shape[:2] + (-1, HD))

def probabilities(queries, key_block, layout):
    key_layout = layout.replace('l', 'm')
    scores = jnp.einsum(layout + ',' + key_layout + '->bhlm', split_heads(queries), split_heads(key_block), precision=lax.Precision.HIGHEST) / math.sqrt(HD)
    length = queries.shape[layout.index('l')]
    causal = lax.broadcasted_iota(jnp.int32, (length, length), 0) >= lax.broadcasted_iota(jnp.int32, (length, length), 1)
    scores = jnp.where(causal, scores, -jnp.inf)
    highest = lax.optimization_barrier(jnp.max(scores, axis=-1, keepdims=True))
    raised = jnp.exp(scores - highest)
    return raised / lax.optimization_barrier(jnp.sum(raised, axis=-1, keepdims=True))

def weighted(probs_all, values, layout):
    key_layout = layout.replace('l', 'm')
    result = jnp.einsum('bhlm,' + key_layout + '->' + layout, rounded(probs_all), split_heads(values), precision=lax.Precision.HIGHEST)
    return result.reshape(values.shape)

def backprop(queries, key_block, values, probs_all, upstream, layout):
    key_layout = layout.replace('l', 'm')
    grad_probs = jnp.einsum(layout + ',' + key_layout + '->bhlm', split_heads(upstream), split_heads(values), precision=lax.Precision.HIGHEST)
    inner = lax.optimization_barrier(jnp.sum(probs_all * grad_probs, axis=-1, keepdims=True))
    grad_scores = rounded(probs_all * (grad_probs - inner) / math.sqrt(HD))
    grad_queries = jnp.einsum('bhlm,' + key_layout + '->' + layout, grad_scores, split_heads(key_block), precision=lax.Precision.HIGHEST)
    grad_keys = jnp.einsum('bhlm,' + layout + '->' + key_layout, grad_scores, split_heads(queries), precision=lax.Precision.HIGHEST)
    grad_values = jnp.einsum('bhlm,' + layout + '->' + key_layout, rounded(probs_all), split_heads(upstream), precision=lax.Precision.HIGHEST)
    return (grad_queries.reshape(queries.shape), grad_keys.reshape(queries.shape), grad_values.reshape(queries.shape))

def normalize(residual, gain):
    stream = residual.astype(jnp.float32)
    inverse = lax.rsqrt(lax.optimization_barrier(jnp.mean(stream * stream, axis=-1, keepdims=True)) + 1e-05)
    return ((stream * inverse * gain.astype(jnp.float32)).astype(jnp.bfloat16), inverse)

def norm_backward(residual, inverse, gain, grad_normed):
    stream = residual.astype(jnp.float32)
    scaled = grad_normed * gain.astype(jnp.float32)
    cubed = inverse * inverse * inverse
    result = inverse * scaled - stream * cubed * lax.optimization_barrier(jnp.mean(stream * scaled, axis=-1, keepdims=True))
    return result.astype(jnp.bfloat16)

def reference(patches, q_rows, k_rows, v_rows, w_out, gain, w_val, q_cols, k_cols, cotangent):

    def step(totals, items):
        patch, query_row, key_row, value_row, query_col, key_col, upstream = items
        probs_rows = probabilities(query_row, key_row, 'blhd')
        attended = weighted(probs_rows, value_row, 'blhd').astype(jnp.bfloat16)
        att_rows = attended.reshape(-1, attended.shape[-1])
        residual = (patch.reshape(-1, D).astype(jnp.float32) + jnp.dot(att_rows, w_out, preferred_element_type=jnp.float32)).astype(jnp.bfloat16)
        normed, inverse = normalize(residual, gain)
        values = jnp.dot(normed, w_val, preferred_element_type=jnp.float32).astype(jnp.bfloat16).reshape(query_col.shape)
        probs_cols = probabilities(query_col, key_col, 'lbhd')
        grad_qcol, grad_kcol, grad_vcol = backprop(query_col, key_col, values, probs_cols, upstream, 'lbhd')
        grad_values = grad_vcol.astype(jnp.bfloat16).reshape(-1, grad_vcol.shape[-1])
        grad_normed = jnp.dot(grad_values, w_val.T, preferred_element_type=jnp.float32)
        grad_stream = norm_backward(residual, inverse, gain, grad_normed)
        grad_att = jnp.dot(grad_stream, w_out.T, preferred_element_type=jnp.float32).astype(jnp.bfloat16).reshape(query_row.shape)
        grad_qrow, grad_krow, grad_vrow = backprop(query_row, key_row, value_row, probs_rows, grad_att, 'blhd')
        new_totals = (totals[0] + jnp.dot(att_rows.T, grad_stream, preferred_element_type=jnp.float32), totals[1] + jnp.dot(normed.T, grad_values, preferred_element_type=jnp.float32))
        outputs = (grad_stream.reshape(patch.shape), grad_qrow.astype(jnp.bfloat16), grad_krow.astype(jnp.bfloat16), grad_vrow.astype(jnp.bfloat16), grad_qcol.astype(jnp.bfloat16), grad_kcol.astype(jnp.bfloat16))
        return (new_totals, outputs)
    start_totals = (jnp.zeros((HW, D), jnp.float32), jnp.zeros((D, HW), jnp.float32))
    totals, outputs = lax.scan(step, start_totals, (patches, q_rows, k_rows, v_rows, q_cols, k_cols, cotangent))
    return (outputs[0], outputs[1], outputs[2], outputs[3], outputs[4], outputs[5], totals[0], totals[1].T.T)
```

```python
import functools
import math

import jax
import jax.numpy as jnp
from jax import lax
from jax.experimental import pallas as pl
from jax.experimental.pallas import tpu as pltpu
from jax.sharding import PartitionSpec as P

HD = 128
HEADS = 8
D = 2048
HW = 1024
T = 256
COPIES = 256
SCALE = 1.0 / math.sqrt(HD)
MESH = pl.DeviceIdType.MESH
F32 = jnp.float32
BF16 = jnp.bfloat16


def dot(a, b, da, db):
    return lax.dot_general(a, b, (((da,), (db,)), ((), ())), preferred_element_type=F32)


def softmax(scores, keep):
    scores = jnp.where(keep, scores * SCALE, -jnp.inf)
    raised = jnp.exp(scores - jnp.max(scores, axis=-1, keepdims=True))
    return raised * (1.0 / jnp.sum(raised, axis=-1, keepdims=True))


def kernel(
    patches, q_rows, k_rows, v_rows, w_out, gain, w_val, q_cols, k_cols, cotangent,
    g_patches, g_qrow, g_krow, g_vrow, g_qcol, g_kcol, g_wout, g_wval,
    Wo, Wv, p_rows, p_cols, att2, gv_col, gv_in, gv_row, gv2, resid, inverse, normed2, scaled,
    val_out, val_in, gp2, g_att,
    Go, Gv, to, tv, so, sv, uo, uv, zo, zv, fo, fv, oo, ov,
    send_sems, recv_sems, local_sems,
):
    x, f, r = lax.axis_index("dp"), lax.axis_index("fsdp"), lax.axis_index("row")
    y, zl, c = r // 4, (r // 2) % 2, r % 2
    z = f * 2 + zl

    def place(px, py, pz, pc):
        return {"dp": px, "fsdp": pz // 2, "row": py * 4 + (pz % 2) * 2 + pc}

    def at_x(k):
        return place((x + k) % 4, y, z, c)

    def at_y(k):
        return place(x, (y + k) % 4, z, c)

    def at_z(k):
        return place(x, y, (z + k) % 8, c)

    def at_row(k):
        return {"dp": x, "fsdp": f, "row": (r + k) % 16}

    sibling = place(x, y, z, 1 - c)

    barrier = pltpu.get_barrier_semaphore()
    peers = [at_row(k) for k in range(1, 16)]
    peers += [place(x, y, ((f + k) % 4) * 2 + s, c) for k in range(1, 4) for s in range(2)]
    peers += [place((x + k) % 4, y, z, s) for k in range(1, 4) for s in range(2)]
    for peer in peers:
        pl.semaphore_signal(barrier, inc=1, device_id=peer, device_id_type=MESH)
    pl.semaphore_wait(barrier, len(peers))

    used = [0]
    sent = []

    def slots(n):
        first = used[0]
        used[0] += n
        assert used[0] <= COPIES
        return first

    def remote(src, dst, where, i):
        return pltpu.make_async_remote_copy(
            src_ref=src, dst_ref=dst, send_sem=send_sems.at[i], recv_sem=recv_sems.at[i],
            device_id=where, device_id_type=MESH,
        )

    def send(src, dst, where, i):
        copy = remote(src, dst, where, i)
        copy.start()
        sent.append(copy)

    def arrived(region, i):
        remote(region, region, sibling, i).wait_recv()

    class Gather:
        def __init__(self, W, own, cols, local):
            self.W, self.own, self.q = W, own, cols // 4
            self.local = local
            self.z, self.two, self.one, self.sib = slots(7), slots(6), slots(12), slots(16)

        def quarter(self, k):
            return pl.ds(pl.multiple_of(((x + k) % 4) * self.q, 128), self.q)

        def start_z(self):
            mine = self.own.at[:, self.quarter(0)]
            there = self.W.at[f, y, zl, c, :, self.quarter(0)]
            self.keep = pltpu.make_async_copy(mine, there, local_sems.at[self.local])
            self.keep.start()
            for k in range(1, 8):
                send(mine, there, at_z(k), self.z + k - 1)

        def start_two(self):
            self.keep.wait()
            for k in range(1, 8):
                pz = (z + 8 - k) % 8
                arrived(self.W.at[pz // 2, y, pz % 2, c, :, self.quarter(0)], self.z + k - 1)
            for part in range(2):
                block = self.W.at[pl.ds(2 * part, 2), y, :, c, :, self.quarter(0)]
                for k in range(1, 4):
                    send(block, block, (at_x if part == 0 else at_y)(k), self.two + 3 * part + k - 1)

        def chunk(self, part, j, k):
            if part == 0:
                return self.W.at[j, (y + k) % 4, :, c, :, :]
            return self.W.at[2 + j, :, :, c, :, self.quarter(k)]

        def other(self, part, j, k):
            if part == 0:
                return self.W.at[j, (y + k) % 4, :, 1 - c, :, :]
            return self.W.at[2 + j, :, :, 1 - c, :, self.quarter(k)]

        def share(self, part, j, k, i):
            block = self.chunk(part, j, k)
            send(block, block, sibling, self.sib + 8 * part + i)

        def start_one(self):
            for part in range(2):
                for k in range(1, 4):
                    if part == 0:
                        region = self.W.at[pl.ds(0, 2), y, :, c, :, self.quarter(4 - k)]
                    else:
                        region = self.W.at[pl.ds(2, 2), (y + 4 - k) % 4, :, c, :, self.quarter(0)]
                    arrived(region, self.two + 3 * part + k - 1)
            for part in range(2):
                at = at_y if part == 0 else at_x
                first = self.one + 6 * part
                a, b = self.chunk(part, 0, 0), self.chunk(part, 1, 0)
                send(a, a, at(1), first)
                send(b, b, at(3), first + 1)
                send(b, b, at(1), first + 2)
                send(a, a, at(3), first + 3)
            for part in range(2):
                self.share(part, 0, 0, 0)
                self.share(part, 1, 0, 1)

        def forward(self):
            for part in range(2):
                at = at_y if part == 0 else at_x
                first = self.one + 6 * part
                a, b = self.chunk(part, 0, 3), self.chunk(part, 1, 1)
                arrived(a, first)
                send(a, a, at(1), first + 4)
                self.share(part, 0, 3, 2)
                arrived(b, first + 1)
                send(b, b, at(3), first + 5)
                self.share(part, 1, 1, 3)

        def nearer(self):
            for part in range(2):
                first = self.one + 6 * part
                arrived(self.chunk(part, 1, 3), first + 2)
                self.share(part, 1, 3, 4)
                arrived(self.chunk(part, 0, 1), first + 3)
                self.share(part, 0, 1, 5)

        def farther(self):
            for part in range(2):
                first = self.one + 6 * part
                arrived(self.chunk(part, 0, 2), first + 4)
                self.share(part, 0, 2, 6)
                arrived(self.chunk(part, 1, 2), first + 5)
                self.share(part, 1, 2, 7)

        def finish(self):
            order = ((0, 0), (1, 0), (0, 3), (1, 1), (1, 3), (0, 1), (0, 2), (1, 2))
            for part in range(2):
                for i, (j, k) in enumerate(order):
                    arrived(self.other(part, j, k), self.sib + 8 * part + i)

    class Scatter:
        def __init__(self, G, t, s, u, zb, fin, o, out, rows, cols, local):
            self.G, self.t, self.s, self.u, self.zb, self.fin, self.o = G, t, s, u, zb, fin, o
            self.out, self.rows, self.q, self.local = out, rows, cols // 8, local
            self.one, self.two, self.three, self.four = slots(12), slots(6), slots(7), slots(7)

        def quarter(self, k):
            return pl.ds(pl.multiple_of(((x + k) % 4) * self.q, 128), self.q)

        def chunk(self, part, j, k):
            if part == 0:
                return self.G.at[j, (y + k) % 4, :, :, :, :]
            return self.G.at[2 + j, :, :, :, :, self.quarter(k)]

        def start_one(self, part):
            at = at_y if part == 0 else at_x
            first = self.one + 6 * part
            t, s = self.t[part], self.s[part]
            send(self.chunk(part, 0, 2), t.at[0], at(1), first)
            send(self.chunk(part, 1, 2), t.at[1], at(3), first + 1)
            send(self.chunk(part, 1, 1), s.at[0, 1], at(1), first + 2)
            send(self.chunk(part, 0, 3), s.at[1, 0], at(3), first + 3)

        def add_into(self, target, others):
            for lead in range(target.shape[0]):
                total = target[lead].astype(F32)
                for other in others:
                    total = total + other[lead].astype(F32)
                target[lead] = total.astype(BF16)

        def merge(self, part):
            at = at_y if part == 0 else at_x
            first = self.one + 6 * part
            t, s = self.t[part], self.s[part]
            arrived(t.at[0], first)
            self.add_into(self.chunk(part, 0, 1), [t.at[0]])
            send(self.chunk(part, 0, 1), s.at[0, 0], at(1), first + 4)
            arrived(t.at[1], first + 1)
            self.add_into(self.chunk(part, 1, 3), [t.at[1]])
            send(self.chunk(part, 1, 3), s.at[1, 1], at(3), first + 5)

        def piece(self, part, k):
            if part == 0:
                return self.G.at[pl.ds(0, 2), y, :, :, :, self.quarter(k)]
            return self.G.at[pl.ds(2, 2), (y + k) % 4, :, :, :, self.quarter(0)]

        def start_two(self, part):
            first = self.one + 6 * part
            s = self.s[part]
            arrived(s.at[0, 1], first + 2)
            arrived(s.at[1, 1], first + 5)
            self.add_into(self.chunk(part, 1, 0), [s.at[0, 1], s.at[1, 1]])
            arrived(s.at[1, 0], first + 3)
            arrived(s.at[0, 0], first + 4)
            self.add_into(self.chunk(part, 0, 0), [s.at[0, 0], s.at[1, 0]])
            for k in range(1, 4):
                send(
                    self.piece(part, k), self.u.at[part, k - 1],
                    (at_x if part == 0 else at_y)(k), self.two + 3 * part + k - 1,
                )

        def end_two(self, part):
            for k in range(1, 4):
                arrived(self.u.at[part, k - 1], self.two + 3 * part + k - 1)
            self.add_into(self.piece(part, 0), [self.u.at[part, k] for k in range(3)])

        def start_three(self):
            for k in range(1, 8):
                pz = (z + k) % 8
                send(
                    self.G.at[pz // 2, y, pz % 2, :, :, self.quarter(0)], self.zb.at[k - 1],
                    at_z(k), self.three + k - 1,
                )

        def start_four(self):
            for k in range(1, 8):
                arrived(self.zb.at[k - 1], self.three + k - 1)
            for pc in range(2):
                total = self.G[f, y, zl, pc, :, self.quarter(0)].astype(F32)
                for k in range(7):
                    total = total + self.zb[k, pc].astype(F32)
                self.fin[pc] = total
            self.keep = pltpu.make_async_copy(
                self.fin.at[c], self.o.at[c, x], local_sems.at[self.local]
            )
            self.keep.start()
            for k in range(4):
                for s in range(2):
                    if k or s:
                        pc = (c + s) % 2
                        send(
                            self.fin.at[pc], self.o.at[c, x], place((x + k) % 4, y, z, pc),
                            self.four + 2 * k + s - 1,
                        )

        def finish(self):
            self.keep.wait()
            for k in range(4):
                for s in range(2):
                    if k or s:
                        arrived(
                            self.o.at[(c + s) % 2, (x + 4 - k) % 4], self.four + 2 * k + s - 1
                        )
            for pc in range(2):
                for px in range(4):
                    first = (4 * pc + px) * self.q
                    self.out[:, first : first + self.q] = self.o[pc, px]

    gather_o = Gather(Wo, w_out, D, 0)
    gather_v = Gather(Wv, w_val, HW, 1)
    scatter_o = Scatter(Go, to, so, uo, zo, fo, oo, g_wout, 16, D, 2)
    scatter_v = Scatter(Gv, tv, sv, uv, zv, fv, ov, g_wval, 32, HW, 3)
    s_gv, s_val, s_act = slots(15), slots(15), slots(4)

    def head(h):
        return pl.ds(pl.multiple_of(h * HD, HD), HD)

    row_keep = lax.broadcasted_iota(jnp.int32, (128, 128), 0) >= lax.broadcasted_iota(
        jnp.int32, (128, 128), 1
    )

    def row_forward(i, _):
        rows, cols = pl.ds(pl.multiple_of((i // HEADS) * 128, 128), 128), head(i % HEADS)
        probs = softmax(dot(q_rows[rows, cols], k_rows[rows, cols], 1, 1), row_keep)
        p_rows[i] = probs
        att2[c, rows, cols] = dot(probs.astype(BF16), v_rows[rows, cols], 1, 0).astype(BF16)
        return 0

    def row_backward(i, _):
        rows, cols = pl.ds(pl.multiple_of((i // HEADS) * 128, 128), 128), head(i % HEADS)
        probs, upstream = p_rows[i], g_att[rows, cols]
        grad = dot(upstream, v_rows[rows, cols], 1, 1)
        inner = jnp.sum(probs * grad, axis=-1, keepdims=True)
        ds = (probs * (grad - inner) * SCALE).astype(BF16)
        g_qrow[rows, cols] = dot(ds, k_rows[rows, cols], 1, 0).astype(BF16)
        g_krow[rows, cols] = dot(ds, q_rows[rows, cols], 0, 0).astype(BF16)
        g_vrow[rows, cols] = dot(probs.astype(BF16), upstream, 0, 0).astype(BF16)
        return 0

    def col_forward(h, _):
        cols = head(h)
        i = lax.broadcasted_iota(jnp.int32, (T, T), 0)
        j = lax.broadcasted_iota(jnp.int32, (T, T), 1)
        keep = (i >= j) & ((i - j) % 8 == 0)
        probs = softmax(dot(q_cols[:, cols], k_cols[:, cols], 1, 1), keep)
        p_cols[h] = probs
        gv_col[:, cols] = dot(probs.astype(BF16), cotangent[:, cols], 0, 0).astype(BF16)
        return 0

    def col_backward(h, _):
        cols = head(h)
        probs = p_cols[h]
        grad = dot(cotangent[:, cols], val_in[:, cols], 1, 1)
        inner = jnp.sum(probs * grad, axis=-1, keepdims=True)
        ds = (probs * (grad - inner) * SCALE).astype(BF16)
        g_qcol[:, cols] = dot(ds, k_cols[:, cols], 1, 0).astype(BF16)
        g_kcol[:, cols] = dot(ds, q_cols[:, cols], 0, 0).astype(BF16)
        return 0

    def block(ref, k):
        return ref.at[pl.ds(pl.multiple_of(((r + k) % 16) * 16, 16), 16)]

    gather_o.start_z()
    gather_v.start_z()
    lax.fori_loop(0, 4, col_forward, 0)
    gather_o.start_two()
    gather_v.start_two()
    lax.fori_loop(4, 8, col_forward, 0)
    for k in range(1, 16):
        send(block(gv_col, k), block(gv_in, 0), at_row(k), s_gv + k - 1)
    keep_gv = pltpu.make_async_copy(block(gv_col, 0), block(gv_in, 0), local_sems.at[4])
    keep_gv.start()
    gather_o.start_one()
    lax.fori_loop(0, 8, row_forward, 0)
    gather_o.forward()
    gather_v.start_one()
    lax.fori_loop(8, 16, row_forward, 0)
    send(att2.at[c], att2.at[c], sibling, s_act)
    gather_o.nearer()

    keep_gv.wait()
    for k in range(1, 16):
        arrived(block(gv_in, 16 - k), s_gv + k - 1)
    for piece in range(0, HW, 256):
        cols = slice(piece, piece + 256)
        moved = gv_in[:, cols].astype(F32).reshape(16, 2, 8, 256)
        for s in range(2):
            gv_row[128 * s : 128 * s + 128, cols] = moved[:, s].reshape(128, 256).astype(BF16)

    def half(k, n):
        return pl.ds(pl.multiple_of(((c + k) % 2) * n, 128), n)

    send(gv_row.at[:, half(1, HW // 2)], gv2.at[c], sibling, s_act + 1)
    gv2[c] = gv_row[:, half(0, HW // 2)]

    gather_o.farther()
    gather_o.finish()

    def residual_tile(i, _):
        cols = pl.ds(pl.multiple_of(i * 512, 512), 512)
        weight = Wo[:, :, :, :, :, cols].reshape(HW, 512)
        resid[:, cols] = (dot(att2[c], weight, 1, 0) + patches[:, cols].astype(F32)).astype(BF16)
        return 0

    lax.fori_loop(0, D // 512, residual_tile, 0)
    gather_v.forward()

    def norm_rows(i, _):
        rows = pl.ds(pl.multiple_of(i * 16, 16), 16)
        stream = resid[rows, :].astype(F32)
        inv = lax.rsqrt(jnp.mean(stream * stream, axis=-1, keepdims=True) + 1e-05)
        inverse[rows, :] = jnp.broadcast_to(inv, (16, 128))
        normed2[c, rows, :] = (stream * inv * gain[...].astype(F32)).astype(BF16)
        return 0

    lax.fori_loop(0, T // 16, norm_rows, 0)
    send(normed2.at[c], normed2.at[c], sibling, s_act + 2)
    gather_v.nearer()
    arrived(gv2.at[1 - c], s_act + 1)
    arrived(normed2.at[1 - c], s_act + 2)

    def wval_tile(i, _):
        left = normed2[:, :, pl.ds(pl.multiple_of(i * 512, 512), 512)].reshape(2 * T, 512)
        Gv[i] = dot(left, gv2[...].reshape(2 * T, 512), 0, 0).astype(BF16).reshape(4, 2, 2, 32, 512)
        return 0

    lax.fori_loop(0, 2, wval_tile, 0)
    scatter_v.start_one(0)
    lax.fori_loop(2, 4, wval_tile, 0)
    scatter_v.start_one(1)
    gather_v.farther()
    gather_v.finish()

    scaled_sum = jnp.zeros((T, 128), F32)

    def normed_grad_tile(i, total):
        cols = pl.ds(pl.multiple_of(i * 512, 512), 512)
        weight = Wv[i].reshape(512, HW)
        grad = dot(gv_row[...], weight, 1, 1) * gain[:, cols].astype(F32)
        scaled[:, cols] = grad
        product = grad * resid[:, cols].astype(F32)
        return total + sum(product[:, 128 * k : 128 * k + 128] for k in range(4))

    scaled_sum = lax.fori_loop(0, 4, normed_grad_tile, scaled_sum)
    scaled[:, D:] = scaled_sum

    def stream_rows(i, _):
        rows = pl.ds(pl.multiple_of(i * 16, 16), 16)
        inv = inverse[rows, 0:1]
        mean = jnp.sum(scaled[rows, D:], axis=-1, keepdims=True) * (1.0 / D)
        stream = resid[rows, :].astype(F32)
        result = inv * scaled[rows, :D] - stream * (inv * inv * inv * mean)
        g_patches[rows, :] = result.astype(BF16)
        return 0

    lax.fori_loop(0, T // 16, stream_rows, 0)
    send(g_patches.at[:, half(1, D // 2)], gp2.at[c], sibling, s_act + 3)
    gp2[c] = g_patches[:, half(0, D // 2)]
    scatter_v.merge(0)
    scatter_v.merge(1)
    arrived(att2.at[1 - c], s_act)
    arrived(gp2.at[1 - c], s_act + 3)

    def wout_tile(i, _):
        left = att2[:, :, pl.ds(pl.multiple_of(i * 256, 256), 256)].reshape(2 * T, 256)
        Go[i] = dot(left, gp2[...].reshape(2 * T, HW), 0, 0).astype(BF16).reshape(4, 2, 2, 16, HW)
        return 0

    lax.fori_loop(0, 2, wout_tile, 0)
    scatter_o.start_one(0)
    lax.fori_loop(2, 4, wout_tile, 0)
    scatter_o.start_one(1)

    def values_tile(i, _):
        cols = pl.ds(pl.multiple_of(i * 256, 256), 256)
        weight = Wv[:, :, :, :, :, cols].reshape(D, 256)
        value = dot(normed2[c], weight, 1, 0).reshape(2, 16, 8, 256)
        both = jnp.concatenate([value[0][:, None], value[1][:, None]], axis=1)
        val_out[:, cols] = both.reshape(T, 256).astype(BF16)
        return 0

    lax.fori_loop(0, HW // 256, values_tile, 0)
    for k in range(1, 16):
        send(block(val_out, k), block(val_in, 0), at_row(k), s_val + k - 1)
    keep_val = pltpu.make_async_copy(block(val_out, 0), block(val_in, 0), local_sems.at[5])
    keep_val.start()

    scatter_v.start_two(0)
    scatter_v.start_two(1)

    def att_grad_tile(i, _):
        weight = Wo[i].reshape(256, D)
        g_att[:, pl.ds(pl.multiple_of(i * 256, 256), 256)] = dot(
            g_patches[...], weight, 1, 1
        ).astype(BF16)
        return 0

    lax.fori_loop(0, 4, att_grad_tile, 0)
    scatter_o.merge(0)
    scatter_o.merge(1)
    lax.fori_loop(0, 8, row_backward, 0)
    scatter_v.end_two(0)
    scatter_v.end_two(1)
    scatter_v.start_three()
    lax.fori_loop(8, 16, row_backward, 0)
    scatter_o.start_two(0)
    scatter_o.start_two(1)
    scatter_v.start_four()
    keep_val.wait()
    for k in range(1, 16):
        arrived(block(val_in, 16 - k), s_val + k - 1)
    lax.fori_loop(0, 4, col_backward, 0)
    scatter_o.end_two(0)
    scatter_o.end_two(1)
    scatter_o.start_three()
    lax.fori_loop(4, 8, col_backward, 0)
    scatter_v.finish()
    scatter_o.start_four()
    scatter_o.finish()
    for copy in sent:
        copy.wait_send()


def body(patches, q_rows, k_rows, v_rows, w_out, gain, w_val, q_cols, k_cols, cotangent):
    vmem = pl.BlockSpec(memory_space=pltpu.VMEM)
    outs = [(T, D), (T, HW), (T, HW), (T, HW), (T, HW), (T, HW)]
    out_shape = [jax.ShapeDtypeStruct(s, BF16) for s in outs]
    out_shape += [jax.ShapeDtypeStruct((16, D), F32), jax.ShapeDtypeStruct((32, HW), F32)]

    def reduce_buffers(rows, cols):
        h, q = cols // 2, cols // 8
        return (
            pltpu.VMEM((4, 4, 2, 2, rows, h), BF16),
            (pltpu.VMEM((2, 2, 2, rows, h), BF16), pltpu.VMEM((2, 4, 2, 2, rows, q), BF16)),
            (pltpu.VMEM((2, 2, 2, 2, rows, h), BF16), pltpu.VMEM((2, 2, 4, 2, 2, rows, q), BF16)),
            pltpu.VMEM((2, 3, 2, 2, 2, rows, q), BF16),
            pltpu.VMEM((7, 2, rows, q), BF16),
            pltpu.VMEM((2, rows, q), F32),
            pltpu.VMEM((2, 4, rows, q), F32),
        )

    ro, rv = reduce_buffers(16, D), reduce_buffers(32, HW)
    scratch = [
        pltpu.VMEM((4, 4, 2, 2, 16, D), BF16),
        pltpu.VMEM((4, 4, 2, 2, 32, HW), BF16),
        pltpu.VMEM((16, 128, 128), F32),
        pltpu.VMEM((HEADS, T, T), F32),
        pltpu.VMEM((2, T, HW), BF16),
        pltpu.VMEM((T, HW), BF16),
        pltpu.VMEM((T, HW), BF16),
        pltpu.VMEM((T, HW), BF16),
        pltpu.VMEM((2, T, HW // 2), BF16),
        pltpu.VMEM((T, D), BF16),
        pltpu.VMEM((T, 128), F32),
        pltpu.VMEM((2, T, D), BF16),
        pltpu.VMEM((T, D + 128), F32),
        pltpu.VMEM((T, HW), BF16),
        pltpu.VMEM((T, HW), BF16),
        pltpu.VMEM((2, T, D // 2), BF16),
        pltpu.VMEM((T, HW), BF16),
    ]
    for a, b in zip(ro, rv):
        scratch += [a, b]
    scratch += [
        pltpu.SemaphoreType.DMA((COPIES,)),
        pltpu.SemaphoreType.DMA((COPIES,)),
        pltpu.SemaphoreType.DMA((6,)),
    ]
    results = pl.pallas_call(
        kernel,
        out_shape=out_shape,
        in_specs=[vmem] * 10,
        out_specs=[vmem] * 8,
        scratch_shapes=scratch,
        compiler_params=pltpu.CompilerParams(
            collective_id=0, has_side_effects=True, vmem_limit_bytes=56 * 2**20
        ),
        name="whole",
    )(
        patches.reshape(T, D), q_rows.reshape(T, HW), k_rows.reshape(T, HW),
        v_rows.reshape(T, HW), w_out, gain.reshape(1, D), w_val, q_cols.reshape(T, HW),
        k_cols.reshape(T, HW), cotangent.reshape(T, HW),
    )
    return (
        results[0].reshape(patches.shape),
        *(results[i].reshape(q_rows.shape) for i in range(1, 4)),
        *(results[i].reshape(q_cols.shape) for i in range(4, 6)),
        results[6],
        results[7],
    )


def solution(mesh):
    rows = P(("dp", "fsdp"), "row", None, None)
    cols = P(("dp", "fsdp"), None, "row", None)
    weights = P(("fsdp", "row"), None)
    return jax.shard_map(
        body,
        mesh=mesh,
        in_specs=(rows, rows, rows, rows, weights, P(), weights, cols, cols, cols),
        out_specs=(rows, rows, rows, rows, cols, cols, weights, weights),
        check_vma=False,
    )
```

```python
import functools
import math

import jax
import jax.numpy as jnp
from jax import lax
from jax.experimental import pallas as pl
from jax.experimental.pallas import tpu as pltpu
from jax.sharding import PartitionSpec as P

HD = 128
HEADS = 8
D = 2048
HW = 1024
T = 256
COPIES = 256
SCALE = 1.0 / math.sqrt(HD)
MESH = pl.DeviceIdType.MESH
F32 = jnp.float32
BF16 = jnp.bfloat16


def dot(a, b, da, db):
    return lax.dot_general(a, b, (((da,), (db,)), ((), ())), preferred_element_type=F32)


def softmax(scores, keep):
    scores = jnp.where(keep, scores * SCALE, -jnp.inf)
    raised = jnp.exp(scores - jnp.max(scores, axis=-1, keepdims=True))
    return raised * (1.0 / jnp.sum(raised, axis=-1, keepdims=True))


def kernel(
    h_patches, h_q_rows, h_k_rows, h_v_rows, h_w_out, h_gain, h_w_val, h_q_cols, h_k_cols, h_cot,
    g_patches, g_qrow, g_krow, g_vrow, g_qcol, g_kcol, g_wout, g_wval,
    Wo, Wv, p_rows, p_cols, att2, gv_col, gv_in, gv_row, gv2, resid, inverse, normed2, scaled,
    val_out, val_in, gp2, g_att,
    Go, Gv, to, tv, so, sv, uo, uv, zo, zv, fo, fv, oo, ov,
    patches, q_rows, k_rows, v_rows, w_out, gain_in, w_val, q_cols, k_cols, cotangent, gain,
    send_sems, recv_sems, local_sems, load_sems,
):
    loads = {}
    for i, (name, source, target) in enumerate((
        ("w_out", h_w_out, w_out), ("w_val", h_w_val, w_val), ("q_cols", h_q_cols, q_cols),
        ("k_cols", h_k_cols, k_cols), ("cotangent", h_cot, cotangent), ("q_rows", h_q_rows, q_rows),
        ("k_rows", h_k_rows, k_rows), ("v_rows", h_v_rows, v_rows), ("gain", h_gain, gain_in),
        ("patches", h_patches, patches),
    )):
        loads[name] = pltpu.make_async_copy(source, target, load_sems.at[i])
        loads[name].start()

    def loaded(*names):
        for name in names:
            loads[name].wait()

    x, f, r = lax.axis_index("dp"), lax.axis_index("fsdp"), lax.axis_index("row")
    y, zl, c = r // 4, (r // 2) % 2, r % 2
    z = f * 2 + zl

    def place(px, py, pz, pc):
        return {"dp": px, "fsdp": pz // 2, "row": py * 4 + (pz % 2) * 2 + pc}

    def at_x(k):
        return place((x + k) % 4, y, z, c)

    def at_y(k):
        return place(x, (y + k) % 4, z, c)

    def at_z(k):
        return place(x, y, (z + k) % 8, c)

    def at_row(k):
        return {"dp": x, "fsdp": f, "row": (r + k) % 16}

    sibling = place(x, y, z, 1 - c)

    barrier = pltpu.get_barrier_semaphore()
    peers = [at_row(k) for k in range(1, 16)]
    peers += [place(x, y, ((f + k) % 4) * 2 + s, c) for k in range(1, 4) for s in range(2)]
    peers += [place((x + k) % 4, y, z, s) for k in range(1, 4) for s in range(2)]
    for peer in peers:
        pl.semaphore_signal(barrier, inc=1, device_id=peer, device_id_type=MESH)
    pl.semaphore_wait(barrier, len(peers))

    used = [0]
    sent = []

    def slots(n):
        first = used[0]
        used[0] += n
        assert used[0] <= COPIES
        return first

    def remote(src, dst, where, i):
        return pltpu.make_async_remote_copy(
            src_ref=src, dst_ref=dst, send_sem=send_sems.at[i], recv_sem=recv_sems.at[i],
            device_id=where, device_id_type=MESH,
        )

    def send(src, dst, where, i):
        copy = remote(src, dst, where, i)
        copy.start()
        sent.append(copy)

    def arrived(region, i):
        remote(region, region, sibling, i).wait_recv()

    class Gather:
        def __init__(self, W, own, cols, local):
            self.W, self.own, self.q = W, own, cols // 4
            self.local = local
            self.z, self.two, self.one, self.sib = slots(7), slots(6), slots(12), slots(16)

        def quarter(self, k):
            return pl.ds(pl.multiple_of(((x + k) % 4) * self.q, 128), self.q)

        def start_z(self):
            mine = self.own.at[:, self.quarter(0)]
            there = self.W.at[f, y, zl, c, :, self.quarter(0)]
            self.keep = pltpu.make_async_copy(mine, there, local_sems.at[self.local])
            self.keep.start()
            for k in range(1, 8):
                send(mine, there, at_z(k), self.z + k - 1)

        def start_two(self):
            self.keep.wait()
            for k in range(1, 8):
                pz = (z + 8 - k) % 8
                arrived(self.W.at[pz // 2, y, pz % 2, c, :, self.quarter(0)], self.z + k - 1)
            for part in range(2):
                block = self.W.at[pl.ds(2 * part, 2), y, :, c, :, self.quarter(0)]
                for k in range(1, 4):
                    send(block, block, (at_x if part == 0 else at_y)(k), self.two + 3 * part + k - 1)

        def chunk(self, part, j, k):
            if part == 0:
                return self.W.at[j, (y + k) % 4, :, c, :, :]
            return self.W.at[2 + j, :, :, c, :, self.quarter(k)]

        def other(self, part, j, k):
            if part == 0:
                return self.W.at[j, (y + k) % 4, :, 1 - c, :, :]
            return self.W.at[2 + j, :, :, 1 - c, :, self.quarter(k)]

        def share(self, part, j, k, i):
            block = self.chunk(part, j, k)
            send(block, block, sibling, self.sib + 8 * part + i)

        def start_one(self):
            for part in range(2):
                for k in range(1, 4):
                    if part == 0:
                        region = self.W.at[pl.ds(0, 2), y, :, c, :, self.quarter(4 - k)]
                    else:
                        region = self.W.at[pl.ds(2, 2), (y + 4 - k) % 4, :, c, :, self.quarter(0)]
                    arrived(region, self.two + 3 * part + k - 1)
            for part in range(2):
                at = at_y if part == 0 else at_x
                first = self.one + 6 * part
                a, b = self.chunk(part, 0, 0), self.chunk(part, 1, 0)
                send(a, a, at(1), first)
                send(b, b, at(3), first + 1)
                send(b, b, at(1), first + 2)
                send(a, a, at(3), first + 3)
            for part in range(2):
                self.share(part, 0, 0, 0)
                self.share(part, 1, 0, 1)

        def forward(self):
            for part in range(2):
                at = at_y if part == 0 else at_x
                first = self.one + 6 * part
                a, b = self.chunk(part, 0, 3), self.chunk(part, 1, 1)
                arrived(a, first)
                send(a, a, at(1), first + 4)
                self.share(part, 0, 3, 2)
                arrived(b, first + 1)
                send(b, b, at(3), first + 5)
                self.share(part, 1, 1, 3)

        def nearer(self):
            for part in range(2):
                first = self.one + 6 * part
                arrived(self.chunk(part, 1, 3), first + 2)
                self.share(part, 1, 3, 4)
                arrived(self.chunk(part, 0, 1), first + 3)
                self.share(part, 0, 1, 5)

        def farther(self):
            for part in range(2):
                first = self.one + 6 * part
                arrived(self.chunk(part, 0, 2), first + 4)
                self.share(part, 0, 2, 6)
                arrived(self.chunk(part, 1, 2), first + 5)
                self.share(part, 1, 2, 7)

        def finish(self):
            order = ((0, 0), (1, 0), (0, 3), (1, 1), (1, 3), (0, 1), (0, 2), (1, 2))
            for part in range(2):
                for i, (j, k) in enumerate(order):
                    arrived(self.other(part, j, k), self.sib + 8 * part + i)

    class Scatter:
        def __init__(self, G, t, s, u, zb, fin, o, out, rows, cols, local):
            self.G, self.t, self.s, self.u, self.zb, self.fin, self.o = G, t, s, u, zb, fin, o
            self.out, self.rows, self.q, self.local = out, rows, cols // 8, local
            self.one, self.two, self.three, self.four = slots(12), slots(6), slots(7), slots(7)

        def quarter(self, k):
            return pl.ds(pl.multiple_of(((x + k) % 4) * self.q, 128), self.q)

        def chunk(self, part, j, k):
            if part == 0:
                return self.G.at[j, (y + k) % 4, :, :, :, :]
            return self.G.at[2 + j, :, :, :, :, self.quarter(k)]

        def start_one(self, part):
            at = at_y if part == 0 else at_x
            first = self.one + 6 * part
            t, s = self.t[part], self.s[part]
            send(self.chunk(part, 0, 2), t.at[0], at(1), first)
            send(self.chunk(part, 1, 2), t.at[1], at(3), first + 1)
            send(self.chunk(part, 1, 1), s.at[0, 1], at(1), first + 2)
            send(self.chunk(part, 0, 3), s.at[1, 0], at(3), first + 3)

        def add_into(self, target, others):
            for lead in range(target.shape[0]):
                total = target[lead].astype(F32)
                for other in others:
                    total = total + other[lead].astype(F32)
                target[lead] = total.astype(BF16)

        def merge(self, part):
            at = at_y if part == 0 else at_x
            first = self.one + 6 * part
            t, s = self.t[part], self.s[part]
            arrived(t.at[0], first)
            self.add_into(self.chunk(part, 0, 1), [t.at[0]])
            send(self.chunk(part, 0, 1), s.at[0, 0], at(1), first + 4)
            arrived(t.at[1], first + 1)
            self.add_into(self.chunk(part, 1, 3), [t.at[1]])
            send(self.chunk(part, 1, 3), s.at[1, 1], at(3), first + 5)

        def piece(self, part, k):
            if part == 0:
                return self.G.at[pl.ds(0, 2), y, :, :, :, self.quarter(k)]
            return self.G.at[pl.ds(2, 2), (y + k) % 4, :, :, :, self.quarter(0)]

        def start_two(self, part):
            first = self.one + 6 * part
            s = self.s[part]
            arrived(s.at[0, 1], first + 2)
            arrived(s.at[1, 1], first + 5)
            self.add_into(self.chunk(part, 1, 0), [s.at[0, 1], s.at[1, 1]])
            arrived(s.at[1, 0], first + 3)
            arrived(s.at[0, 0], first + 4)
            self.add_into(self.chunk(part, 0, 0), [s.at[0, 0], s.at[1, 0]])
            for k in range(1, 4):
                send(
                    self.piece(part, k), self.u.at[part, k - 1],
                    (at_x if part == 0 else at_y)(k), self.two + 3 * part + k - 1,
                )

        def end_two(self, part):
            for k in range(1, 4):
                arrived(self.u.at[part, k - 1], self.two + 3 * part + k - 1)
            self.add_into(self.piece(part, 0), [self.u.at[part, k] for k in range(3)])

        def start_three(self):
            for k in range(1, 8):
                pz = (z + k) % 8
                send(
                    self.G.at[pz // 2, y, pz % 2, :, :, self.quarter(0)], self.zb.at[k - 1],
                    at_z(k), self.three + k - 1,
                )

        def start_four(self):
            for k in range(1, 8):
                arrived(self.zb.at[k - 1], self.three + k - 1)
            for pc in range(2):
                total = self.G[f, y, zl, pc, :, self.quarter(0)].astype(F32)
                for k in range(7):
                    total = total + self.zb[k, pc].astype(F32)
                self.fin[pc] = total
            self.keep = pltpu.make_async_copy(
                self.fin.at[c], self.o.at[c, x], local_sems.at[self.local]
            )
            self.keep.start()
            for k in range(4):
                for s in range(2):
                    if k or s:
                        pc = (c + s) % 2
                        send(
                            self.fin.at[pc], self.o.at[c, x], place((x + k) % 4, y, z, pc),
                            self.four + 2 * k + s - 1,
                        )

        def finish(self):
            self.keep.wait()
            for k in range(4):
                for s in range(2):
                    if k or s:
                        arrived(
                            self.o.at[(c + s) % 2, (x + 4 - k) % 4], self.four + 2 * k + s - 1
                        )
            for pc in range(2):
                for px in range(4):
                    first = (4 * pc + px) * self.q
                    self.out[:, first : first + self.q] = self.o[pc, px]

    gather_o = Gather(Wo, w_out, D, 0)
    gather_v = Gather(Wv, w_val, HW, 1)
    scatter_o = Scatter(Go, to, so, uo, zo, fo, oo, g_wout, 16, D, 2)
    scatter_v = Scatter(Gv, tv, sv, uv, zv, fv, ov, g_wval, 32, HW, 3)
    s_gv, s_val, s_act = slots(15), slots(15), slots(4)

    def head(h):
        return pl.ds(pl.multiple_of(h * HD, HD), HD)

    row_keep = lax.broadcasted_iota(jnp.int32, (128, 128), 0) >= lax.broadcasted_iota(
        jnp.int32, (128, 128), 1
    )

    def row_forward(i, _):
        rows, cols = pl.ds(pl.multiple_of((i // HEADS) * 128, 128), 128), head(i % HEADS)
        probs = softmax(dot(q_rows[rows, cols], k_rows[rows, cols], 1, 1), row_keep)
        p_rows[i] = probs
        att2[c, rows, cols] = dot(probs.astype(BF16), v_rows[rows, cols], 1, 0).astype(BF16)
        return 0

    def row_backward(i, _):
        rows, cols = pl.ds(pl.multiple_of((i // HEADS) * 128, 128), 128), head(i % HEADS)
        probs, upstream = p_rows[i], g_att[rows, cols]
        grad = dot(upstream, v_rows[rows, cols], 1, 1)
        inner = jnp.sum(probs * grad, axis=-1, keepdims=True)
        ds = (probs * (grad - inner) * SCALE).astype(BF16)
        g_qrow[rows, cols] = dot(ds, k_rows[rows, cols], 1, 0).astype(BF16)
        g_krow[rows, cols] = dot(ds, q_rows[rows, cols], 0, 0).astype(BF16)
        g_vrow[rows, cols] = dot(probs.astype(BF16), upstream, 0, 0).astype(BF16)
        return 0

    def col_forward(h, _):
        cols = head(h)
        i = lax.broadcasted_iota(jnp.int32, (T, T), 0)
        j = lax.broadcasted_iota(jnp.int32, (T, T), 1)
        keep = (i >= j) & ((i - j) % 8 == 0)
        probs = softmax(dot(q_cols[:, cols], k_cols[:, cols], 1, 1), keep)
        p_cols[h] = probs
        gv_col[:, cols] = dot(probs.astype(BF16), cotangent[:, cols], 0, 0).astype(BF16)
        return 0

    def col_backward(h, _):
        cols = head(h)
        probs = p_cols[h]
        grad = dot(cotangent[:, cols], val_in[:, cols], 1, 1)
        inner = jnp.sum(probs * grad, axis=-1, keepdims=True)
        ds = (probs * (grad - inner) * SCALE).astype(BF16)
        g_qcol[:, cols] = dot(ds, k_cols[:, cols], 1, 0).astype(BF16)
        g_kcol[:, cols] = dot(ds, q_cols[:, cols], 0, 0).astype(BF16)
        return 0

    def block(ref, k):
        return ref.at[pl.ds(pl.multiple_of(((r + k) % 16) * 16, 16), 16)]

    def rows_forward(i):
        if i == 0:
            loaded("q_rows", "k_rows", "v_rows")
        lax.fori_loop(4 * i, 4 * i + 4, row_forward, 0, unroll=4)

    def cols_forward(i):
        if i == 0:
            loaded("q_cols", "k_cols", "cotangent")
        lax.fori_loop(2 * i, 2 * i + 2, col_forward, 0, unroll=2)

    def rows_backward(i):
        lax.fori_loop(4 * i, 4 * i + 4, row_backward, 0, unroll=4)

    def cols_backward(i):
        lax.fori_loop(2 * i, 2 * i + 2, col_backward, 0, unroll=2)

    keep_gv = pltpu.make_async_copy(block(gv_col, 0), block(gv_in, 0), local_sems.at[4])
    keep_val = pltpu.make_async_copy(block(val_out, 0), block(val_in, 0), local_sems.at[5])

    def send_gv():
        for k in range(1, 16):
            send(block(gv_col, k), block(gv_in, 0), at_row(k), s_gv + k - 1)
        keep_gv.start()

    def half(k, n):
        return pl.ds(pl.multiple_of(((c + k) % 2) * n, 128), n)

    def take_gv():
        keep_gv.wait()
        for k in range(1, 16):
            arrived(block(gv_in, 16 - k), s_gv + k - 1)
        for piece in range(0, HW, 256):
            cols = slice(piece, piece + 256)
            moved = gv_in[:, cols].astype(F32).reshape(16, 2, 8, 256)
            for s in range(2):
                gv_row[128 * s : 128 * s + 128, cols] = moved[:, s].reshape(128, 256).astype(BF16)
        send(gv_row.at[:, half(1, HW // 2)], gv2.at[c], sibling, s_act + 1)
        gv2[c] = gv_row[:, half(0, HW // 2)]

    def send_att():
        send(att2.at[c], att2.at[c], sibling, s_act)

    def residual_tile(i, _):
        cols = pl.ds(pl.multiple_of(i * 512, 512), 512)
        weight = Wo[:, :, :, :, :, cols].reshape(HW, 512)
        resid[:, cols] = (dot(att2[c], weight, 1, 0) + patches[:, cols].astype(F32)).astype(BF16)
        return 0

    def residual():
        loaded("patches")
        lax.fori_loop(0, D // 512, residual_tile, 0)

    def norm_rows(i, _):
        rows = pl.ds(pl.multiple_of(i * 16, 16), 16)
        stream = resid[rows, :].astype(F32)
        inv = lax.rsqrt(jnp.mean(stream * stream, axis=-1, keepdims=True) + 1e-05)
        inverse[rows, :] = jnp.broadcast_to(inv, (16, 128))
        normed2[c, rows, :] = (stream * inv * gain[...]).astype(BF16)
        return 0

    def norm():
        loaded("gain")
        gain_rows = gain_in[...].astype(F32)
        for i in range(D // 128):
            gain[:, 128 * i : 128 * i + 128] = gain_rows[i : i + 1, :]
        lax.fori_loop(0, T // 16, norm_rows, 0, unroll=4)
        send(normed2.at[c], normed2.at[c], sibling, s_act + 2)

    def wval_tile(i, _):
        left = normed2[:, :, pl.ds(pl.multiple_of(i * 512, 512), 512)].reshape(2 * T, 512)
        Gv[i] = dot(left, gv2[...].reshape(2 * T, 512), 0, 0).astype(BF16).reshape(4, 2, 2, 32, 512)
        return 0

    def wval(part):
        if part == 0:
            arrived(gv2.at[1 - c], s_act + 1)
            arrived(normed2.at[1 - c], s_act + 2)
        lax.fori_loop(2 * part, 2 * part + 2, wval_tile, 0)
        scatter_v.start_one(part)

    def normed_grad_tile(i, total):
        cols = pl.ds(pl.multiple_of(i * 512, 512), 512)
        weight = Wv[i].reshape(512, HW)
        grad = dot(gv_row[...], weight, 1, 1) * gain[:, cols]
        scaled[:, cols] = grad
        product = grad * resid[:, cols].astype(F32)
        return total + sum(product[:, 128 * k : 128 * k + 128] for k in range(4))

    def normed_grad():
        scaled[:, D:] = lax.fori_loop(0, 4, normed_grad_tile, jnp.zeros((T, 128), F32))

    def stream_rows(i, _):
        rows = pl.ds(pl.multiple_of(i * 16, 16), 16)
        inv = inverse[rows, 0:1]
        mean = jnp.sum(scaled[rows, D:], axis=-1, keepdims=True) * (1.0 / D)
        stream = resid[rows, :].astype(F32)
        result = inv * scaled[rows, :D] - stream * (inv * inv * inv * mean)
        g_patches[rows, :] = result.astype(BF16)
        return 0

    def stream_grad():
        lax.fori_loop(0, T // 16, stream_rows, 0, unroll=4)
        send(g_patches.at[:, half(1, D // 2)], gp2.at[c], sibling, s_act + 3)
        gp2[c] = g_patches[:, half(0, D // 2)]

    def wout_tile(i, _):
        left = att2[:, :, pl.ds(pl.multiple_of(i * 256, 256), 256)].reshape(2 * T, 256)
        Go[i] = dot(left, gp2[...].reshape(2 * T, HW), 0, 0).astype(BF16).reshape(4, 2, 2, 16, HW)
        return 0

    def wout(part):
        if part == 0:
            arrived(att2.at[1 - c], s_act)
            arrived(gp2.at[1 - c], s_act + 3)
        lax.fori_loop(2 * part, 2 * part + 2, wout_tile, 0)
        scatter_o.start_one(part)

    def values_tile(i, _):
        cols = pl.ds(pl.multiple_of(i * 256, 256), 256)
        weight = Wv[:, :, :, :, :, cols].reshape(D, 256)
        value = dot(normed2[c], weight, 1, 0).reshape(2, 16, 8, 256)
        both = jnp.concatenate([value[0][:, None], value[1][:, None]], axis=1)
        val_out[:, cols] = both.reshape(T, 256).astype(BF16)
        return 0

    def send_values():
        lax.fori_loop(0, HW // 256, values_tile, 0)
        for k in range(1, 16):
            send(block(val_out, k), block(val_in, 0), at_row(k), s_val + k - 1)
        keep_val.start()

    def take_values():
        keep_val.wait()
        for k in range(1, 16):
            arrived(block(val_in, 16 - k), s_val + k - 1)

    def att_grad_tile(i, _):
        weight = Wo[i].reshape(256, D)
        g_att[:, pl.ds(pl.multiple_of(i * 256, 256), 256)] = dot(
            g_patches[...], weight, 1, 1
        ).astype(BF16)
        return 0

    def att_grad():
        lax.fori_loop(0, 4, att_grad_tile, 0)

    loaded("w_val")
    gather_v.start_z()
    rows_forward(0)
    rows_forward(1)
    loaded("w_out")
    gather_o.start_z()
    cols_forward(0)
    gather_v.start_two()
    gather_o.start_two()
    rows_forward(2)
    gather_v.start_one()
    cols_forward(1)
    gather_o.start_one()
    rows_forward(3)
    gather_o.forward()
    cols_forward(2)
    gather_o.nearer()
    gather_v.forward()
    cols_forward(3)
    gather_o.farther()
    send_gv()
    gather_v.nearer()
    send_att()
    gather_v.farther()
    gather_o.finish()
    residual()
    norm()
    gather_v.finish()
    send_values()
    take_gv()
    normed_grad()
    wval(0)
    wval(1)
    stream_grad()
    wout(0)
    wout(1)
    att_grad()
    scatter_v.merge(1)
    scatter_v.merge(0)
    scatter_o.merge(0)
    scatter_o.merge(1)
    rows_backward(0)
    take_values()
    scatter_v.start_two(1)
    scatter_v.start_two(0)
    rows_backward(1)
    scatter_o.start_two(1)
    scatter_o.start_two(0)
    scatter_v.end_two(1)
    scatter_v.end_two(0)
    scatter_v.start_three()
    cols_backward(0)
    scatter_o.end_two(1)
    scatter_o.end_two(0)
    scatter_o.start_three()
    cols_backward(1)
    rows_backward(2)
    scatter_v.start_four()
    cols_backward(2)
    scatter_o.start_four()
    rows_backward(3)
    cols_backward(3)
    scatter_o.finish()
    scatter_v.finish()
    for copy in sent:
        copy.wait_send()


def place_results(*refs):
    copies = [pltpu.make_async_copy(refs[i], refs[8 + i], refs[16].at[i]) for i in range(8)]
    for copy in copies:
        copy.start()
    for copy in copies:
        copy.wait()


def body(patches, q_rows, k_rows, v_rows, w_out, gain, w_val, q_cols, k_cols, cotangent):
    vmem = pl.BlockSpec(memory_space=pltpu.VMEM)
    outs = [(T, D), (T, HW), (T, HW), (T, HW), (T, HW), (T, HW)]
    out_shape = [jax.ShapeDtypeStruct(s, BF16) for s in outs]
    out_shape += [jax.ShapeDtypeStruct((16, D), F32), jax.ShapeDtypeStruct((32, HW), F32)]

    def reduce_buffers(rows, cols):
        h, q = cols // 2, cols // 8
        return (
            pltpu.VMEM((4, 4, 2, 2, rows, h), BF16),
            (pltpu.VMEM((2, 2, 2, rows, h), BF16), pltpu.VMEM((2, 4, 2, 2, rows, q), BF16)),
            (pltpu.VMEM((2, 2, 2, 2, rows, h), BF16), pltpu.VMEM((2, 2, 4, 2, 2, rows, q), BF16)),
            pltpu.VMEM((2, 3, 2, 2, 2, rows, q), BF16),
            pltpu.VMEM((7, 2, rows, q), BF16),
            pltpu.VMEM((2, rows, q), F32),
            pltpu.VMEM((2, 4, rows, q), F32),
        )

    ro, rv = reduce_buffers(16, D), reduce_buffers(32, HW)
    scratch = [
        pltpu.VMEM((4, 4, 2, 2, 16, D), BF16),
        pltpu.VMEM((4, 4, 2, 2, 32, HW), BF16),
        pltpu.VMEM((16, 128, 128), F32),
        pltpu.VMEM((HEADS, T, T), F32),
        pltpu.VMEM((2, T, HW), BF16),
        pltpu.VMEM((T, HW), BF16),
        pltpu.VMEM((T, HW), BF16),
        pltpu.VMEM((T, HW), BF16),
        pltpu.VMEM((2, T, HW // 2), BF16),
        pltpu.VMEM((T, D), BF16),
        pltpu.VMEM((T, 128), F32),
        pltpu.VMEM((2, T, D), BF16),
        pltpu.VMEM((T, D + 128), F32),
        pltpu.VMEM((T, HW), BF16),
        pltpu.VMEM((T, HW), BF16),
        pltpu.VMEM((2, T, D // 2), BF16),
        pltpu.VMEM((T, HW), BF16),
    ]
    for a, b in zip(ro, rv):
        scratch += [a, b]
    inputs = [(T, D), (T, HW), (T, HW), (T, HW), (16, D), (D // 128, 128), (32, HW)] + [(T, HW)] * 3
    scratch += [pltpu.VMEM(shape, BF16) for shape in inputs] + [pltpu.VMEM((1, D), F32)]
    scratch += [
        pltpu.SemaphoreType.DMA((COPIES,)),
        pltpu.SemaphoreType.DMA((COPIES,)),
        pltpu.SemaphoreType.DMA((6,)),
        pltpu.SemaphoreType.DMA((10,)),
    ]
    operands = (
        patches.reshape(T, D), q_rows.reshape(T, HW), k_rows.reshape(T, HW),
        v_rows.reshape(T, HW), w_out, gain.reshape(D // 128, 128), w_val, q_cols.reshape(T, HW),
        k_cols.reshape(T, HW), cotangent.reshape(T, HW),
    )
    operands = [pltpu.with_memory_space_constraint(a, pltpu.HBM) for a in operands]
    results = pl.pallas_call(
        kernel,
        out_shape=out_shape,
        in_specs=[pl.BlockSpec(memory_space=pltpu.HBM)] * 10,
        out_specs=[vmem] * 8,
        scratch_shapes=scratch,
        compiler_params=pltpu.CompilerParams(
            collective_id=0, has_side_effects=True, vmem_limit_bytes=46 * 2**20
        ),
        name="whole",
    )(*operands)
    anywhere = pl.BlockSpec(memory_space=pl.ANY)
    results = pl.pallas_call(
        place_results,
        out_shape=out_shape,
        in_specs=[anywhere] * 8,
        out_specs=[pl.BlockSpec(memory_space=pltpu.HBM)] * 8,
        scratch_shapes=[pltpu.SemaphoreType.DMA((8,))],
        compiler_params=pltpu.CompilerParams(vmem_limit_bytes=2**20),
        name="place",
    )(*results)
    return (
        results[0].reshape(patches.shape),
        *(results[i].reshape(q_rows.shape) for i in range(1, 4)),
        *(results[i].reshape(q_cols.shape) for i in range(4, 6)),
        results[6],
        results[7],
    )


def solution(mesh):
    rows = P(("dp", "fsdp"), "row", None, None)
    cols = P(("dp", "fsdp"), None, "row", None)
    weights = P(("fsdp", "row"), None)
    return jax.shard_map(
        body,
        mesh=mesh,
        in_specs=(rows, rows, rows, rows, weights, P(), weights, cols, cols, cols),
        out_specs=(rows, rows, rows, rows, cols, cols, weights, weights),
        check_vma=False,
    )
```

```python
import functools
import math

import jax
import jax.numpy as jnp
from jax import lax
from jax.experimental import pallas as pl
from jax.experimental.pallas import tpu as pltpu
from jax.sharding import PartitionSpec as P

HD = 128
HEADS = 8
D = 2048
HW = 1024
T = 256
SENDS = 26
RECVS = 72
SCALE = 1.0 / math.sqrt(HD)
MESH = pl.DeviceIdType.MESH
F32 = jnp.float32
BF16 = jnp.bfloat16


def dot(a, b, da, db):
    return lax.dot_general(a, b, (((da,), (db,)), ((), ())), preferred_element_type=F32)


def softmax(scores, keep):
    scores = jnp.where(keep, scores * SCALE, -jnp.inf)
    raised = jnp.exp(scores - jnp.max(scores, axis=-1, keepdims=True))
    return raised * (1.0 / jnp.sum(raised, axis=-1, keepdims=True))


def kernel(
    h_patches, h_q_rows, h_k_rows, h_v_rows, h_w_out, h_gain, h_w_val, h_q_cols, h_k_cols, h_cot,
    g_patches, g_qrow, g_krow, g_vrow, g_qcol, g_kcol, g_wout, g_wval,
    Wo, Wv, p_rows, p_cols, att2, gv_col, gv_in, gv_row, gv2, resid, inverse, normed2, scaled,
    val_out, val_in, gp2, g_att,
    Go, Gv, to, tv, so, sv, uo, uv, zo, zv, fo, fv, oo, ov,
    patches, q_rows, k_rows, v_rows, w_out, gain_in, w_val, q_cols, k_cols, cotangent, gain, spare,
    send_sems, recv_sems, local_sems, load_sems,
):
    loads = {}
    for i, (name, source, target) in enumerate((
        ("w_out", h_w_out, w_out), ("w_val", h_w_val, w_val), ("q_cols", h_q_cols, q_cols),
        ("k_cols", h_k_cols, k_cols), ("cotangent", h_cot, cotangent), ("q_rows", h_q_rows, q_rows),
        ("k_rows", h_k_rows, k_rows), ("v_rows", h_v_rows, v_rows), ("gain", h_gain, gain_in),
        ("patches", h_patches, patches),
    )):
        loads[name] = pltpu.make_async_copy(source, target, load_sems.at[i])
        loads[name].start()

    def loaded(*names):
        for name in names:
            loads[name].wait()

    x, f, r = lax.axis_index("dp"), lax.axis_index("fsdp"), lax.axis_index("row")
    y, zl, c = r // 4, (r // 2) % 2, r % 2
    z = f * 2 + zl

    def place(px, py, pz, pc):
        return {"dp": px, "fsdp": pz // 2, "row": py * 4 + (pz % 2) * 2 + pc}

    def at_x(k):
        return place((x + k) % 4, y, z, c)

    def at_y(k):
        return place(x, (y + k) % 4, z, c)

    def at_z(k):
        return place(x, y, (z + k) % 8, c)

    def at_row(k):
        return {"dp": x, "fsdp": f, "row": (r + k) % 16}

    sibling = place(x, y, z, 1 - c)

    barrier = pltpu.get_barrier_semaphore()
    peers = [at_row(k) for k in range(1, 16)]
    peers += [place(x, y, ((f + k) % 4) * 2 + s, c) for k in range(1, 4) for s in range(2)]
    peers += [place((x + k) % 4, y, z, s) for k in range(1, 4) for s in range(2)]
    for peer in peers:
        pl.semaphore_signal(barrier, inc=1, device_id=peer, device_id_type=MESH)
    pl.semaphore_wait(barrier, len(peers))

    counts = {"send": 0, "recv": 0}
    sent = {}

    def slots(kind, n):
        first = counts[kind]
        counts[kind] += n
        assert counts[kind] <= (SENDS if kind == "send" else RECVS)
        return first

    def remote(src, dst, where, i, g):
        return pltpu.make_async_remote_copy(
            src_ref=src, dst_ref=dst, send_sem=send_sems.at[g], recv_sem=recv_sems.at[i],
            device_id=where, device_id_type=MESH,
        )

    def size(ref):
        return math.prod(ref.shape) * jnp.dtype(ref.dtype).itemsize

    def send(src, dst, where, i, g):
        remote(src, dst, where, i, g).start()
        sent[g] = sent.get(g, 0) + size(src)

    def span(total):
        assert total % 4096 == 0 and total <= 2**20
        return spare.at[0 : total // 256]

    def arrived(region, i):
        remote(region, region, sibling, i, 0).wait_recv()

    def all_arrived(total, i):
        remote(span(total), span(total), sibling, i, 0).wait_recv()

    class Gather:
        def __init__(self, W, own, cols, local):
            self.W, self.own, self.q = W, own, cols // 4
            self.local = local
            self.z, self.two = slots("recv", 1), slots("recv", 2)
            self.one, self.sib = slots("recv", 12), slots("recv", 2)
            self.sz, self.s1, self.ss = slots("send", 1), slots("send", 2), slots("send", 2)
            self.block = size(own)

        def quarter(self, k):
            return pl.ds(pl.multiple_of(((x + k) % 4) * self.q, 128), self.q)

        def start_z(self):
            mine = self.own.at[:, self.quarter(0)]
            there = self.W.at[f, y, zl, c, :, self.quarter(0)]
            self.keep = pltpu.make_async_copy(mine, there, local_sems.at[self.local])
            self.keep.start()
            for k in range(1, 8):
                send(mine, there, at_z(k), self.z, self.sz)

        def start_two(self):
            self.keep.wait()
            all_arrived(7 * self.block // 4, self.z)
            for part in range(2):
                block = self.W.at[pl.ds(2 * part, 2), y, :, c, :, self.quarter(0)]
                for k in range(1, 4):
                    send(block, block, (at_x if part == 0 else at_y)(k), self.two + part, self.sz)

        def chunk(self, part, j, k):
            if part == 0:
                return self.W.at[j, (y + k) % 4, :, c, :, :]
            return self.W.at[2 + j, :, :, c, :, self.quarter(k)]

        def share(self, part, j, k):
            block = self.chunk(part, j, k)
            send(block, block, sibling, self.sib + part, self.ss + part)

        def start_one(self):
            for part in range(2):
                all_arrived(3 * self.block, self.two + part)
            for part in range(2):
                at = at_y if part == 0 else at_x
                first = self.one + 6 * part
                a, b = self.chunk(part, 0, 0), self.chunk(part, 1, 0)
                send(a, a, at(1), first, self.s1 + part)
                send(b, b, at(3), first + 1, self.s1 + part)
                send(b, b, at(1), first + 2, self.s1 + part)
                send(a, a, at(3), first + 3, self.s1 + part)
            for part in range(2):
                self.share(part, 0, 0)
                self.share(part, 1, 0)

        def forward(self):
            for part in range(2):
                at = at_y if part == 0 else at_x
                first = self.one + 6 * part
                a, b = self.chunk(part, 0, 3), self.chunk(part, 1, 1)
                arrived(a, first)
                send(a, a, at(1), first + 4, self.s1 + part)
                self.share(part, 0, 3)
                arrived(b, first + 1)
                send(b, b, at(3), first + 5, self.s1 + part)
                self.share(part, 1, 1)

        def nearer(self):
            for part in range(2):
                first = self.one + 6 * part
                arrived(self.chunk(part, 1, 3), first + 2)
                self.share(part, 1, 3)
                arrived(self.chunk(part, 0, 1), first + 3)
                self.share(part, 0, 1)

        def farther(self):
            for part in range(2):
                first = self.one + 6 * part
                arrived(self.chunk(part, 0, 2), first + 4)
                self.share(part, 0, 2)
                arrived(self.chunk(part, 1, 2), first + 5)
                self.share(part, 1, 2)

        def finish(self):
            for part in range(2):
                all_arrived(16 * self.block, self.sib + part)

    class Scatter:
        def __init__(self, G, t, s, u, zb, fin, o, out, rows, cols, local):
            self.G, self.t, self.s, self.u, self.zb, self.fin, self.o = G, t, s, u, zb, fin, o
            self.out, self.rows, self.q, self.local = out, rows, cols // 8, local
            self.one, self.two = slots("recv", 12), slots("recv", 2)
            self.three, self.four = slots("recv", 1), slots("recv", 1)
            self.s1, self.s2 = slots("send", 2), slots("send", 1)
            self.s3, self.s4 = slots("send", 1), slots("send", 1)
            self.block = 2 * rows * cols

        def quarter(self, k):
            return pl.ds(pl.multiple_of(((x + k) % 4) * self.q, 128), self.q)

        def chunk(self, part, j, k):
            if part == 0:
                return self.G.at[j, (y + k) % 4, :, :, :, :]
            return self.G.at[2 + j, :, :, :, :, self.quarter(k)]

        def start_one(self, part):
            at = at_y if part == 0 else at_x
            first = self.one + 6 * part
            t, s = self.t[part], self.s[part]
            send(self.chunk(part, 0, 2), t.at[0], at(1), first, self.s1 + part)
            send(self.chunk(part, 1, 2), t.at[1], at(3), first + 1, self.s1 + part)
            send(self.chunk(part, 1, 1), s.at[0, 1], at(1), first + 2, self.s1 + part)
            send(self.chunk(part, 0, 3), s.at[1, 0], at(3), first + 3, self.s1 + part)

        def add_into(self, target, others):
            for lead in range(target.shape[0]):
                total = target[lead].astype(F32)
                for other in others:
                    total = total + other[lead].astype(F32)
                target[lead] = total.astype(BF16)

        def merge(self, part):
            at = at_y if part == 0 else at_x
            first = self.one + 6 * part
            t, s = self.t[part], self.s[part]
            arrived(t.at[0], first)
            self.add_into(self.chunk(part, 0, 1), [t.at[0]])
            send(self.chunk(part, 0, 1), s.at[0, 0], at(1), first + 4, self.s1 + part)
            arrived(t.at[1], first + 1)
            self.add_into(self.chunk(part, 1, 3), [t.at[1]])
            send(self.chunk(part, 1, 3), s.at[1, 1], at(3), first + 5, self.s1 + part)

        def piece(self, part, k):
            if part == 0:
                return self.G.at[pl.ds(0, 2), y, :, :, :, self.quarter(k)]
            return self.G.at[pl.ds(2, 2), (y + k) % 4, :, :, :, self.quarter(0)]

        def start_two(self, part):
            first = self.one + 6 * part
            s = self.s[part]
            arrived(s.at[0, 1], first + 2)
            arrived(s.at[1, 1], first + 5)
            self.add_into(self.chunk(part, 1, 0), [s.at[0, 1], s.at[1, 1]])
            arrived(s.at[1, 0], first + 3)
            arrived(s.at[0, 0], first + 4)
            self.add_into(self.chunk(part, 0, 0), [s.at[0, 0], s.at[1, 0]])
            for k in range(1, 4):
                send(
                    self.piece(part, k), self.u.at[part, k - 1],
                    (at_x if part == 0 else at_y)(k), self.two + part, self.s2,
                )

        def end_two(self, part):
            all_arrived(3 * self.block, self.two + part)
            self.add_into(self.piece(part, 0), [self.u.at[part, k] for k in range(3)])

        def start_three(self):
            for k in range(1, 8):
                pz = (z + k) % 8
                send(
                    self.G.at[pz // 2, y, pz % 2, :, :, self.quarter(0)], self.zb.at[k - 1],
                    at_z(k), self.three, self.s3,
                )

        def start_four(self):
            all_arrived(7 * self.block // 4, self.three)
            for pc in range(2):
                total = self.G[f, y, zl, pc, :, self.quarter(0)].astype(F32)
                for k in range(7):
                    total = total + self.zb[k, pc].astype(F32)
                self.fin[pc] = total
            self.keep = pltpu.make_async_copy(
                self.fin.at[c], self.o.at[c, x], local_sems.at[self.local]
            )
            self.keep.start()
            for k in range(4):
                for s in range(2):
                    if k or s:
                        pc = (c + s) % 2
                        send(
                            self.fin.at[pc], self.o.at[c, x], place((x + k) % 4, y, z, pc),
                            self.four, self.s4,
                        )

        def finish(self):
            self.keep.wait()
            all_arrived(7 * self.block // 4, self.four)
            for pc in range(2):
                for px in range(4):
                    first = (4 * pc + px) * self.q
                    self.out[:, first : first + self.q] = self.o[pc, px]

    gather_o = Gather(Wo, w_out, D, 0)
    gather_v = Gather(Wv, w_val, HW, 1)
    scatter_o = Scatter(Go, to, so, uo, zo, fo, oo, g_wout, 16, D, 2)
    scatter_v = Scatter(Gv, tv, sv, uv, zv, fv, ov, g_wval, 32, HW, 3)
    s_gv, s_val, s_act = slots("recv", 1), slots("recv", 1), slots("recv", 4)
    t_gv, t_val, t_act = slots("send", 1), slots("send", 1), slots("send", 4)

    def head(h):
        return pl.ds(pl.multiple_of(h * HD, HD), HD)

    row_keep = lax.broadcasted_iota(jnp.int32, (128, 128), 0) >= lax.broadcasted_iota(
        jnp.int32, (128, 128), 1
    )

    def row_forward(i, _):
        rows, cols = pl.ds(pl.multiple_of((i // HEADS) * 128, 128), 128), head(i % HEADS)
        probs = softmax(dot(q_rows[rows, cols], k_rows[rows, cols], 1, 1), row_keep)
        p_rows[i] = probs
        att2[c, rows, cols] = dot(probs.astype(BF16), v_rows[rows, cols], 1, 0).astype(BF16)
        return 0

    def row_backward(i, _):
        rows, cols = pl.ds(pl.multiple_of((i // HEADS) * 128, 128), 128), head(i % HEADS)
        probs, upstream = p_rows[i], g_att[rows, cols]
        grad = dot(upstream, v_rows[rows, cols], 1, 1)
        inner = jnp.sum(probs * grad, axis=-1, keepdims=True)
        ds = (probs * (grad - inner) * SCALE).astype(BF16)
        g_qrow[rows, cols] = dot(ds, k_rows[rows, cols], 1, 0).astype(BF16)
        g_krow[rows, cols] = dot(ds, q_rows[rows, cols], 0, 0).astype(BF16)
        g_vrow[rows, cols] = dot(probs.astype(BF16), upstream, 0, 0).astype(BF16)
        return 0

    def col_forward(h, _):
        cols = head(h)
        i = lax.broadcasted_iota(jnp.int32, (T, T), 0)
        j = lax.broadcasted_iota(jnp.int32, (T, T), 1)
        keep = (i >= j) & ((i - j) % 8 == 0)
        probs = softmax(dot(q_cols[:, cols], k_cols[:, cols], 1, 1), keep)
        p_cols[h] = probs
        gv_col[:, cols] = dot(probs.astype(BF16), cotangent[:, cols], 0, 0).astype(BF16)
        return 0

    def col_backward(h, _):
        cols = head(h)
        probs = p_cols[h]
        grad = dot(cotangent[:, cols], val_in[:, cols], 1, 1)
        inner = jnp.sum(probs * grad, axis=-1, keepdims=True)
        ds = (probs * (grad - inner) * SCALE).astype(BF16)
        g_qcol[:, cols] = dot(ds, k_cols[:, cols], 1, 0).astype(BF16)
        g_kcol[:, cols] = dot(ds, q_cols[:, cols], 0, 0).astype(BF16)
        return 0

    def block(ref, k):
        return ref.at[pl.ds(pl.multiple_of(((r + k) % 16) * 16, 16), 16)]

    def rows_forward(i):
        if i == 0:
            loaded("q_rows", "k_rows", "v_rows")
        lax.fori_loop(4 * i, 4 * i + 4, row_forward, 0, unroll=4)

    def cols_forward(i):
        if i == 0:
            loaded("q_cols", "k_cols", "cotangent")
        lax.fori_loop(2 * i, 2 * i + 2, col_forward, 0, unroll=2)

    def rows_backward(i):
        lax.fori_loop(4 * i, 4 * i + 4, row_backward, 0, unroll=4)

    def cols_backward(i):
        lax.fori_loop(2 * i, 2 * i + 2, col_backward, 0, unroll=2)

    keep_gv = pltpu.make_async_copy(block(gv_col, 0), block(gv_in, 0), local_sems.at[4])
    keep_val = pltpu.make_async_copy(block(val_out, 0), block(val_in, 0), local_sems.at[5])

    def send_gv():
        for k in range(1, 16):
            send(block(gv_col, k), block(gv_in, 0), at_row(k), s_gv, t_gv)
        keep_gv.start()

    def half(k, n):
        return pl.ds(pl.multiple_of(((c + k) % 2) * n, 128), n)

    def take_gv():
        keep_gv.wait()
        all_arrived(15 * 32 * HW, s_gv)
        for piece in range(0, HW, 256):
            cols = slice(piece, piece + 256)
            moved = gv_in[:, cols].astype(F32).reshape(16, 2, 8, 256)
            for s in range(2):
                gv_row[128 * s : 128 * s + 128, cols] = moved[:, s].reshape(128, 256).astype(BF16)
        send(gv_row.at[:, half(1, HW // 2)], gv2.at[c], sibling, s_act + 1, t_act + 1)
        gv2[c] = gv_row[:, half(0, HW // 2)]

    def send_att():
        send(att2.at[c], att2.at[c], sibling, s_act, t_act)

    def residual_tile(i, _):
        cols = pl.ds(pl.multiple_of(i * 512, 512), 512)
        weight = Wo[:, :, :, :, :, cols].reshape(HW, 512)
        resid[:, cols] = (dot(att2[c], weight, 1, 0) + patches[:, cols].astype(F32)).astype(BF16)
        return 0

    def residual():
        loaded("patches")
        lax.fori_loop(0, D // 512, residual_tile, 0)

    def norm_rows(i, _):
        rows = pl.ds(pl.multiple_of(i * 16, 16), 16)
        stream = resid[rows, :].astype(F32)
        inv = lax.rsqrt(jnp.mean(stream * stream, axis=-1, keepdims=True) + 1e-05)
        inverse[rows, :] = jnp.broadcast_to(inv, (16, 128))
        normed2[c, rows, :] = (stream * inv * gain[...]).astype(BF16)
        return 0

    def norm():
        loaded("gain")
        gain_rows = gain_in[...].astype(F32)
        for i in range(D // 128):
            gain[:, 128 * i : 128 * i + 128] = gain_rows[i : i + 1, :]
        lax.fori_loop(0, T // 16, norm_rows, 0, unroll=4)
        send(normed2.at[c], normed2.at[c], sibling, s_act + 2, t_act + 2)

    def wval_tile(i, _):
        left = normed2[:, :, pl.ds(pl.multiple_of(i * 512, 512), 512)].reshape(2 * T, 512)
        Gv[i] = dot(left, gv2[...].reshape(2 * T, 512), 0, 0).astype(BF16).reshape(4, 2, 2, 32, 512)
        return 0

    def wval(part):
        if part == 0:
            arrived(gv2.at[1 - c], s_act + 1)
            arrived(normed2.at[1 - c], s_act + 2)
        lax.fori_loop(2 * part, 2 * part + 2, wval_tile, 0)
        scatter_v.start_one(part)

    def normed_grad_tile(i, total):
        cols = pl.ds(pl.multiple_of(i * 512, 512), 512)
        weight = Wv[i].reshape(512, HW)
        grad = dot(gv_row[...], weight, 1, 1) * gain[:, cols]
        scaled[:, cols] = grad
        product = grad * resid[:, cols].astype(F32)
        return total + sum(product[:, 128 * k : 128 * k + 128] for k in range(4))

    def normed_grad():
        scaled[:, D:] = lax.fori_loop(0, 4, normed_grad_tile, jnp.zeros((T, 128), F32))

    def stream_rows(i, _):
        rows = pl.ds(pl.multiple_of(i * 16, 16), 16)
        inv = inverse[rows, 0:1]
        mean = jnp.sum(scaled[rows, D:], axis=-1, keepdims=True) * (1.0 / D)
        stream = resid[rows, :].astype(F32)
        result = inv * scaled[rows, :D] - stream * (inv * inv * inv * mean)
        g_patches[rows, :] = result.astype(BF16)
        return 0

    def stream_grad():
        lax.fori_loop(0, T // 16, stream_rows, 0, unroll=4)
        send(g_patches.at[:, half(1, D // 2)], gp2.at[c], sibling, s_act + 3, t_act + 3)
        gp2[c] = g_patches[:, half(0, D // 2)]

    def wout_tile(i, _):
        left = att2[:, :, pl.ds(pl.multiple_of(i * 256, 256), 256)].reshape(2 * T, 256)
        Go[i] = dot(left, gp2[...].reshape(2 * T, HW), 0, 0).astype(BF16).reshape(4, 2, 2, 16, HW)
        return 0

    def wout(part):
        if part == 0:
            arrived(att2.at[1 - c], s_act)
            arrived(gp2.at[1 - c], s_act + 3)
        lax.fori_loop(2 * part, 2 * part + 2, wout_tile, 0)
        scatter_o.start_one(part)

    def values_tile(i, _):
        cols = pl.ds(pl.multiple_of(i * 256, 256), 256)
        weight = Wv[:, :, :, :, :, cols].reshape(D, 256)
        value = dot(normed2[c], weight, 1, 0).reshape(2, 16, 8, 256)
        both = jnp.concatenate([value[0][:, None], value[1][:, None]], axis=1)
        val_out[:, cols] = both.reshape(T, 256).astype(BF16)
        return 0

    def send_values():
        lax.fori_loop(0, HW // 256, values_tile, 0)
        for k in range(1, 16):
            send(block(val_out, k), block(val_in, 0), at_row(k), s_val, t_val)
        keep_val.start()

    def take_values():
        keep_val.wait()
        all_arrived(15 * 32 * HW, s_val)

    def att_grad_tile(i, _):
        weight = Wo[i].reshape(256, D)
        g_att[:, pl.ds(pl.multiple_of(i * 256, 256), 256)] = dot(
            g_patches[...], weight, 1, 1
        ).astype(BF16)
        return 0

    def att_grad():
        lax.fori_loop(0, 4, att_grad_tile, 0)

    loaded("w_val")
    gather_v.start_z()
    rows_forward(0)
    rows_forward(1)
    loaded("w_out")
    gather_o.start_z()
    cols_forward(0)
    gather_v.start_two()
    gather_o.start_two()
    rows_forward(2)
    gather_v.start_one()
    cols_forward(1)
    gather_o.start_one()
    rows_forward(3)
    gather_o.forward()
    cols_forward(2)
    gather_o.nearer()
    gather_v.forward()
    cols_forward(3)
    gather_o.farther()
    send_gv()
    gather_v.nearer()
    send_att()
    gather_v.farther()
    gather_o.finish()
    residual()
    norm()
    gather_v.finish()
    send_values()
    take_gv()
    normed_grad()
    wval(0)
    wval(1)
    stream_grad()
    wout(0)
    wout(1)
    att_grad()
    scatter_v.merge(1)
    scatter_v.merge(0)
    scatter_o.merge(0)
    scatter_o.merge(1)
    rows_backward(0)
    take_values()
    scatter_v.start_two(1)
    scatter_v.start_two(0)
    rows_backward(1)
    scatter_o.start_two(1)
    scatter_o.start_two(0)
    scatter_v.end_two(1)
    scatter_v.end_two(0)
    scatter_v.start_three()
    cols_backward(0)
    scatter_o.end_two(1)
    scatter_o.end_two(0)
    scatter_o.start_three()
    cols_backward(1)
    rows_backward(2)
    scatter_v.start_four()
    cols_backward(2)
    scatter_o.start_four()
    rows_backward(3)
    cols_backward(3)
    scatter_o.finish()
    scatter_v.finish()
    for g, total in sent.items():
        remote(span(total), span(total), sibling, 0, g).wait_send()


def place_results(*refs):
    copies = [pltpu.make_async_copy(refs[i], refs[8 + i], refs[16].at[i]) for i in range(8)]
    for copy in copies:
        copy.start()
    for copy in copies:
        copy.wait()


def body(patches, q_rows, k_rows, v_rows, w_out, gain, w_val, q_cols, k_cols, cotangent):
    vmem = pl.BlockSpec(memory_space=pltpu.VMEM)
    outs = [(T, D), (T, HW), (T, HW), (T, HW), (T, HW), (T, HW)]
    out_shape = [jax.ShapeDtypeStruct(s, BF16) for s in outs]
    out_shape += [jax.ShapeDtypeStruct((16, D), F32), jax.ShapeDtypeStruct((32, HW), F32)]

    def reduce_buffers(rows, cols):
        h, q = cols // 2, cols // 8
        return (
            pltpu.VMEM((4, 4, 2, 2, rows, h), BF16),
            (pltpu.VMEM((2, 2, 2, rows, h), BF16), pltpu.VMEM((2, 4, 2, 2, rows, q), BF16)),
            (pltpu.VMEM((2, 2, 2, 2, rows, h), BF16), pltpu.VMEM((2, 2, 4, 2, 2, rows, q), BF16)),
            pltpu.VMEM((2, 3, 2, 2, 2, rows, q), BF16),
            pltpu.VMEM((7, 2, rows, q), BF16),
            pltpu.VMEM((2, rows, q), F32),
            pltpu.VMEM((2, 4, rows, q), F32),
        )

    ro, rv = reduce_buffers(16, D), reduce_buffers(32, HW)
    scratch = [
        pltpu.VMEM((4, 4, 2, 2, 16, D), BF16),
        pltpu.VMEM((4, 4, 2, 2, 32, HW), BF16),
        pltpu.VMEM((16, 128, 128), F32),
        pltpu.VMEM((HEADS, T, T), F32),
        pltpu.VMEM((2, T, HW), BF16),
        pltpu.VMEM((T, HW), BF16),
        pltpu.VMEM((T, HW), BF16),
        pltpu.VMEM((T, HW), BF16),
        pltpu.VMEM((2, T, HW // 2), BF16),
        pltpu.VMEM((T, D), BF16),
        pltpu.VMEM((T, 128), F32),
        pltpu.VMEM((2, T, D), BF16),
        pltpu.VMEM((T, D + 128), F32),
        pltpu.VMEM((T, HW), BF16),
        pltpu.VMEM((T, HW), BF16),
        pltpu.VMEM((2, T, D // 2), BF16),
        pltpu.VMEM((T, HW), BF16),
    ]
    for a, b in zip(ro, rv):
        scratch += [a, b]
    inputs = [(T, D), (T, HW), (T, HW), (T, HW), (16, D), (D // 128, 128), (32, HW)] + [(T, HW)] * 3
    scratch += [pltpu.VMEM(shape, BF16) for shape in inputs] + [pltpu.VMEM((1, D), F32), pltpu.VMEM((4096, 128), BF16)]
    scratch += [
        pltpu.SemaphoreType.DMA((SENDS,)),
        pltpu.SemaphoreType.DMA((RECVS,)),
        pltpu.SemaphoreType.DMA((6,)),
        pltpu.SemaphoreType.DMA((10,)),
    ]
    operands = (
        patches.reshape(T, D), q_rows.reshape(T, HW), k_rows.reshape(T, HW),
        v_rows.reshape(T, HW), w_out, gain.reshape(D // 128, 128), w_val, q_cols.reshape(T, HW),
        k_cols.reshape(T, HW), cotangent.reshape(T, HW),
    )
    operands = [pltpu.with_memory_space_constraint(a, pltpu.HBM) for a in operands]
    results = pl.pallas_call(
        kernel,
        out_shape=out_shape,
        in_specs=[pl.BlockSpec(memory_space=pltpu.HBM)] * 10,
        out_specs=[vmem] * 8,
        scratch_shapes=scratch,
        compiler_params=pltpu.CompilerParams(
            collective_id=0, has_side_effects=True, vmem_limit_bytes=46 * 2**20
        ),
        name="whole",
    )(*operands)
    anywhere = pl.BlockSpec(memory_space=pl.ANY)
    results = pl.pallas_call(
        place_results,
        out_shape=out_shape,
        in_specs=[anywhere] * 8,
        out_specs=[pl.BlockSpec(memory_space=pltpu.HBM)] * 8,
        scratch_shapes=[pltpu.SemaphoreType.DMA((8,))],
        compiler_params=pltpu.CompilerParams(vmem_limit_bytes=2**20),
        name="place",
    )(*results)
    return (
        results[0].reshape(patches.shape),
        *(results[i].reshape(q_rows.shape) for i in range(1, 4)),
        *(results[i].reshape(q_cols.shape) for i in range(4, 6)),
        results[6],
        results[7],
    )


def solution(mesh):
    rows = P(("dp", "fsdp"), "row", None, None)
    cols = P(("dp", "fsdp"), None, "row", None)
    weights = P(("fsdp", "row"), None)
    return jax.shard_map(
        body,
        mesh=mesh,
        in_specs=(rows, rows, rows, rows, weights, P(), weights, cols, cols, cols),
        out_specs=(rows, rows, rows, rows, cols, cols, weights, weights),
        check_vma=False,
    )
```

```python
import functools
import math

import jax
import jax.numpy as jnp
from jax import lax
from jax.experimental import pallas as pl
from jax.experimental.pallas import tpu as pltpu
from jax.sharding import PartitionSpec as P

HD = 128
HEADS = 8
D = 2048
HW = 1024
T = 256
SENDS = 26
RECVS = 72
SCALE = 1.0 / math.sqrt(HD)
MESH = pl.DeviceIdType.MESH
F32 = jnp.float32
BF16 = jnp.bfloat16


def dot(a, b, da, db):
    return lax.dot_general(a, b, (((da,), (db,)), ((), ())), preferred_element_type=F32)


def softmax(scores, keep):
    scores = jnp.where(keep, scores * SCALE, -jnp.inf)
    raised = jnp.exp(scores - jnp.max(scores, axis=-1, keepdims=True))
    return raised * (1.0 / jnp.sum(raised, axis=-1, keepdims=True))


def kernel(
    h_patches, h_q_rows, h_k_rows, h_v_rows, h_w_out, h_gain, h_w_val, h_q_cols, h_k_cols, h_cot,
    g_patches, g_qrow, g_krow, g_vrow, g_qcol, g_kcol, g_wout, g_wval,
    Wo, Wv, p_rows, p_cols, att2, gv_col, gv_in, gv_row, gv2, resid, inverse, normed2, scaled,
    val_out, val_in, gp2, g_att,
    Go, Gv, to, tv, so, sv, uo, uv, zo, zv, fo, fv, oo, ov,
    patches, q_rows, k_rows, v_rows, w_out, gain_in, w_val, q_cols, k_cols, cotangent, gain, spare,
    send_sems, recv_sems, local_sems, load_sems,
):
    loads = {}
    for i, (name, source, target) in enumerate((
        ("w_out", h_w_out, w_out), ("w_val", h_w_val, w_val), ("q_cols", h_q_cols, q_cols),
        ("k_cols", h_k_cols, k_cols), ("cotangent", h_cot, cotangent), ("q_rows", h_q_rows, q_rows),
        ("k_rows", h_k_rows, k_rows), ("v_rows", h_v_rows, v_rows), ("gain", h_gain, gain_in),
        ("patches", h_patches, patches),
    )):
        loads[name] = pltpu.make_async_copy(source, target, load_sems.at[i])
        loads[name].start()

    def loaded(*names):
        for name in names:
            loads[name].wait()

    x, f, r = lax.axis_index("dp"), lax.axis_index("fsdp"), lax.axis_index("row")
    y, zl, c = r // 4, (r // 2) % 2, r % 2
    z = f * 2 + zl

    def place(px, py, pz, pc):
        return {"dp": px, "fsdp": pz // 2, "row": py * 4 + (pz % 2) * 2 + pc}

    def at_x(k):
        return place((x + k) % 4, y, z, c)

    def at_y(k):
        return place(x, (y + k) % 4, z, c)

    def at_z(k):
        return place(x, y, (z + k) % 8, c)

    def at_row(k):
        return {"dp": x, "fsdp": f, "row": (r + k) % 16}

    sibling = place(x, y, z, 1 - c)

    barrier = pltpu.get_barrier_semaphore()
    peers = [at_row(k) for k in range(1, 16)]
    peers += [place(x, y, ((f + k) % 4) * 2 + s, c) for k in range(1, 4) for s in range(2)]
    peers += [place((x + k) % 4, y, z, s) for k in range(1, 4) for s in range(2)]
    for peer in peers:
        pl.semaphore_signal(barrier, inc=1, device_id=peer, device_id_type=MESH)
    pl.semaphore_wait(barrier, len(peers))

    counts = {"send": 0, "recv": 0}
    sent = {}

    def slots(kind, n):
        first = counts[kind]
        counts[kind] += n
        assert counts[kind] <= (SENDS if kind == "send" else RECVS)
        return first

    def remote(src, dst, where, i, g):
        return pltpu.make_async_remote_copy(
            src_ref=src, dst_ref=dst, send_sem=send_sems.at[g], recv_sem=recv_sems.at[i],
            device_id=where, device_id_type=MESH,
        )

    def size(ref):
        return math.prod(ref.shape) * jnp.dtype(ref.dtype).itemsize

    def send(src, dst, where, i, g):
        remote(src, dst, where, i, g).start()
        sent[g] = sent.get(g, 0) + size(src)

    def span(total):
        assert total % 4096 == 0 and total <= 2**20
        return spare.at[0 : total // 256]

    def arrived(region, i):
        remote(region, region, sibling, i, 0).wait_recv()

    def all_arrived(total, i):
        remote(span(total), span(total), sibling, i, 0).wait_recv()

    class Gather:
        def __init__(self, W, own, cols, local):
            self.W, self.own, self.q = W, own, cols // 4
            self.local = local
            self.z, self.two = slots("recv", 1), slots("recv", 2)
            self.one, self.sib = slots("recv", 12), slots("recv", 2)
            self.sz, self.s1, self.ss = slots("send", 1), slots("send", 2), slots("send", 2)
            self.block = size(own)

        def quarter(self, k):
            return pl.ds(pl.multiple_of(((x + k) % 4) * self.q, 128), self.q)

        def start_z(self):
            mine = self.own.at[:, self.quarter(0)]
            there = self.W.at[f, y, zl, c, :, self.quarter(0)]
            self.keep = pltpu.make_async_copy(mine, there, local_sems.at[self.local])
            self.keep.start()
            for k in range(1, 8):
                send(mine, there, at_z(k), self.z, self.sz)

        def start_two(self):
            self.keep.wait()
            all_arrived(7 * self.block // 4, self.z)
            for part in range(2):
                block = self.W.at[pl.ds(2 * part, 2), y, :, c, :, self.quarter(0)]
                for k in range(1, 4):
                    send(block, block, (at_x if part == 0 else at_y)(k), self.two + part, self.sz)

        def chunk(self, part, j, k):
            if part == 0:
                return self.W.at[j, (y + k) % 4, :, c, :, :]
            return self.W.at[2 + j, :, :, c, :, self.quarter(k)]

        def share(self, part, j, k):
            block = self.chunk(part, j, k)
            send(block, block, sibling, self.sib + part, self.ss + part)

        def start_one(self):
            for part in range(2):
                all_arrived(3 * self.block, self.two + part)
            for part in range(2):
                at = at_y if part == 0 else at_x
                first = self.one + 6 * part
                a, b = self.chunk(part, 0, 0), self.chunk(part, 1, 0)
                send(a, a, at(1), first, self.s1 + part)
                send(b, b, at(3), first + 1, self.s1 + part)
                send(b, b, at(1), first + 2, self.s1 + part)
                send(a, a, at(3), first + 3, self.s1 + part)
            for part in range(2):
                self.share(part, 0, 0)
                self.share(part, 1, 0)

        def forward(self):
            for part in range(2):
                at = at_y if part == 0 else at_x
                first = self.one + 6 * part
                a, b = self.chunk(part, 0, 3), self.chunk(part, 1, 1)
                arrived(a, first)
                send(a, a, at(1), first + 4, self.s1 + part)
                self.share(part, 0, 3)
                arrived(b, first + 1)
                send(b, b, at(3), first + 5, self.s1 + part)
                self.share(part, 1, 1)

        def nearer(self):
            for part in range(2):
                first = self.one + 6 * part
                arrived(self.chunk(part, 1, 3), first + 2)
                self.share(part, 1, 3)
                arrived(self.chunk(part, 0, 1), first + 3)
                self.share(part, 0, 1)

        def farther(self):
            for part in range(2):
                first = self.one + 6 * part
                arrived(self.chunk(part, 0, 2), first + 4)
                self.share(part, 0, 2)
                arrived(self.chunk(part, 1, 2), first + 5)
                self.share(part, 1, 2)

        def finish(self):
            for part in range(2):
                all_arrived(16 * self.block, self.sib + part)

    class Scatter:
        def __init__(self, G, t, s, u, zb, fin, o, out, rows, cols, local):
            self.G, self.t, self.s, self.u, self.zb, self.fin, self.o = G, t, s, u, zb, fin, o
            self.out, self.rows, self.q, self.local = out, rows, cols // 8, local
            self.one, self.two = slots("recv", 12), slots("recv", 2)
            self.three, self.four = slots("recv", 1), slots("recv", 1)
            self.s1, self.s2 = slots("send", 2), slots("send", 1)
            self.s3, self.s4 = slots("send", 1), slots("send", 1)
            self.block = 2 * rows * cols

        def quarter(self, k):
            return pl.ds(pl.multiple_of(((x + k) % 4) * self.q, 128), self.q)

        def chunk(self, part, j, k):
            if part == 0:
                return self.G.at[j, (y + k) % 4, :, :, :, :]
            return self.G.at[2 + j, :, :, :, :, self.quarter(k)]

        def start_one(self, part):
            at = at_y if part == 0 else at_x
            first = self.one + 6 * part
            t, s = self.t[part], self.s[part]
            send(self.chunk(part, 0, 2), t.at[0], at(1), first, self.s1 + part)
            send(self.chunk(part, 1, 2), t.at[1], at(3), first + 1, self.s1 + part)
            send(self.chunk(part, 1, 1), s.at[0, 1], at(1), first + 2, self.s1 + part)
            send(self.chunk(part, 0, 3), s.at[1, 0], at(3), first + 3, self.s1 + part)

        def add_into(self, target, others):
            for lead in range(target.shape[0]):
                total = target[lead].astype(F32)
                for other in others:
                    total = total + other[lead].astype(F32)
                target[lead] = total.astype(BF16)

        def merge(self, part):
            at = at_y if part == 0 else at_x
            first = self.one + 6 * part
            t, s = self.t[part], self.s[part]
            arrived(t.at[0], first)
            self.add_into(self.chunk(part, 0, 1), [t.at[0]])
            send(self.chunk(part, 0, 1), s.at[0, 0], at(1), first + 4, self.s1 + part)
            arrived(t.at[1], first + 1)
            self.add_into(self.chunk(part, 1, 3), [t.at[1]])
            send(self.chunk(part, 1, 3), s.at[1, 1], at(3), first + 5, self.s1 + part)

        def piece(self, part, k):
            if part == 0:
                return self.G.at[pl.ds(0, 2), y, :, :, :, self.quarter(k)]
            return self.G.at[pl.ds(2, 2), (y + k) % 4, :, :, :, self.quarter(0)]

        def start_two(self, part):
            first = self.one + 6 * part
            s = self.s[part]
            arrived(s.at[0, 1], first + 2)
            arrived(s.at[1, 1], first + 5)
            self.add_into(self.chunk(part, 1, 0), [s.at[0, 1], s.at[1, 1]])
            arrived(s.at[1, 0], first + 3)
            arrived(s.at[0, 0], first + 4)
            self.add_into(self.chunk(part, 0, 0), [s.at[0, 0], s.at[1, 0]])
            for k in range(1, 4):
                send(
                    self.piece(part, k), self.u.at[part, k - 1],
                    (at_x if part == 0 else at_y)(k), self.two + part, self.s2,
                )

        def end_two(self, part):
            all_arrived(3 * self.block, self.two + part)
            self.add_into(self.piece(part, 0), [self.u.at[part, k] for k in range(3)])

        def start_three(self):
            for k in range(1, 8):
                pz = (z + k) % 8
                send(
                    self.G.at[pz // 2, y, pz % 2, :, :, self.quarter(0)], self.zb.at[k - 1],
                    at_z(k), self.three, self.s3,
                )

        def start_four(self):
            all_arrived(7 * self.block // 4, self.three)
            for pc in range(2):
                total = self.G[f, y, zl, pc, :, self.quarter(0)].astype(F32)
                for k in range(7):
                    total = total + self.zb[k, pc].astype(F32)
                self.fin[pc] = total
            self.keep = pltpu.make_async_copy(
                self.fin.at[c], self.o.at[c, x], local_sems.at[self.local]
            )
            self.keep.start()
            for k in range(4):
                for s in range(2):
                    if k or s:
                        pc = (c + s) % 2
                        send(
                            self.fin.at[pc], self.o.at[c, x], place((x + k) % 4, y, z, pc),
                            self.four, self.s4,
                        )

        def finish(self):
            self.keep.wait()
            all_arrived(7 * self.block // 4, self.four)
            for pc in range(2):
                for px in range(4):
                    first = (4 * pc + px) * self.q
                    self.out[:, first : first + self.q] = self.o[pc, px]

    gather_o = Gather(Wo, w_out, D, 0)
    gather_v = Gather(Wv, w_val, HW, 1)
    scatter_o = Scatter(Go, to, so, uo, zo, fo, oo, g_wout, 16, D, 2)
    scatter_v = Scatter(Gv, tv, sv, uv, zv, fv, ov, g_wval, 32, HW, 3)
    s_gv, s_val, s_act = slots("recv", 1), slots("recv", 1), slots("recv", 4)
    t_gv, t_val, t_act = slots("send", 1), slots("send", 1), slots("send", 4)

    def head(h):
        return pl.ds(pl.multiple_of(h * HD, HD), HD)

    row_keep = lax.broadcasted_iota(jnp.int32, (128, 128), 0) >= lax.broadcasted_iota(
        jnp.int32, (128, 128), 1
    )

    def row_forward(i, _):
        rows, cols = pl.ds(pl.multiple_of((i // HEADS) * 128, 128), 128), head(i % HEADS)
        probs = softmax(dot(q_rows[rows, cols], k_rows[rows, cols], 1, 1), row_keep)
        p_rows[i] = probs
        att2[c, rows, cols] = dot(probs.astype(BF16), v_rows[rows, cols], 1, 0).astype(BF16)
        return 0

    def row_backward(i, _):
        rows, cols = pl.ds(pl.multiple_of((i // HEADS) * 128, 128), 128), head(i % HEADS)
        probs, upstream = p_rows[i], g_att[rows, cols]
        grad = dot(upstream, v_rows[rows, cols], 1, 1)
        inner = jnp.sum(probs * grad, axis=-1, keepdims=True)
        ds = (probs * (grad - inner) * SCALE).astype(BF16)
        g_qrow[rows, cols] = dot(ds, k_rows[rows, cols], 1, 0).astype(BF16)
        g_krow[rows, cols] = dot(ds, q_rows[rows, cols], 0, 0).astype(BF16)
        g_vrow[rows, cols] = dot(probs.astype(BF16), upstream, 0, 0).astype(BF16)
        return 0

    def col_forward(h, _):
        cols = head(h)
        i = lax.broadcasted_iota(jnp.int32, (T, T), 0)
        j = lax.broadcasted_iota(jnp.int32, (T, T), 1)
        keep = (i >= j) & ((i - j) % 8 == 0)
        probs = softmax(dot(q_cols[:, cols], k_cols[:, cols], 1, 1), keep)
        p_cols[h] = probs
        gv_col[:, cols] = dot(probs.astype(BF16), cotangent[:, cols], 0, 0).astype(BF16)
        return 0

    def col_backward(h, _):
        cols = head(h)
        probs = p_cols[h]
        grad = dot(cotangent[:, cols], val_in[:, cols], 1, 1)
        inner = jnp.sum(probs * grad, axis=-1, keepdims=True)
        ds = (probs * (grad - inner) * SCALE).astype(BF16)
        g_qcol[:, cols] = dot(ds, k_cols[:, cols], 1, 0).astype(BF16)
        g_kcol[:, cols] = dot(ds, q_cols[:, cols], 0, 0).astype(BF16)
        return 0

    def block(ref, k):
        return ref.at[pl.ds(pl.multiple_of(((r + k) % 16) * 16, 16), 16)]

    def rows_forward(i):
        if i == 0:
            loaded("q_rows", "k_rows", "v_rows")
        lax.fori_loop(4 * i, 4 * i + 4, row_forward, 0, unroll=4)

    def cols_forward(i):
        if i == 0:
            loaded("q_cols", "k_cols", "cotangent")
        lax.fori_loop(2 * i, 2 * i + 2, col_forward, 0, unroll=2)

    def rows_backward(i):
        lax.fori_loop(4 * i, 4 * i + 4, row_backward, 0, unroll=4)

    def cols_backward(i):
        lax.fori_loop(2 * i, 2 * i + 2, col_backward, 0, unroll=2)

    keep_gv = pltpu.make_async_copy(block(gv_col, 0), block(gv_in, 0), local_sems.at[4])
    keep_val = pltpu.make_async_copy(block(val_out, 0), block(val_in, 0), local_sems.at[5])

    def send_gv():
        for k in range(1, 16):
            send(block(gv_col, k), block(gv_in, 0), at_row(k), s_gv, t_gv)
        keep_gv.start()

    def half(k, n):
        return pl.ds(pl.multiple_of(((c + k) % 2) * n, 128), n)

    def take_gv():
        keep_gv.wait()
        all_arrived(15 * 32 * HW, s_gv)
        for piece in range(0, HW, 256):
            cols = slice(piece, piece + 256)
            moved = gv_in[:, cols].astype(F32).reshape(16, 2, 8, 256)
            for s in range(2):
                gv_row[128 * s : 128 * s + 128, cols] = moved[:, s].reshape(128, 256).astype(BF16)
        send(gv_row.at[:, half(1, HW // 2)], gv2.at[c], sibling, s_act + 1, t_act + 1)
        gv2[c] = gv_row[:, half(0, HW // 2)]

    def send_att():
        send(att2.at[c], att2.at[c], sibling, s_act, t_act)

    def residual_tile(i, _):
        cols = pl.ds(pl.multiple_of(i * 512, 512), 512)
        weight = Wo[:, :, :, :, :, cols].reshape(HW, 512)
        resid[:, cols] = (dot(att2[c], weight, 1, 0) + patches[:, cols].astype(F32)).astype(BF16)
        return 0

    def residual():
        loaded("patches")
        lax.fori_loop(0, D // 512, residual_tile, 0)

    def norm_rows(i, _):
        rows = pl.ds(pl.multiple_of(i * 16, 16), 16)
        stream = resid[rows, :].astype(F32)
        inv = lax.rsqrt(jnp.mean(stream * stream, axis=-1, keepdims=True) + 1e-05)
        inverse[rows, :] = jnp.broadcast_to(inv, (16, 128))
        normed2[c, rows, :] = (stream * inv * gain[...]).astype(BF16)
        return 0

    def norm():
        loaded("gain")
        gain_rows = gain_in[...].astype(F32)
        for i in range(D // 128):
            gain[:, 128 * i : 128 * i + 128] = gain_rows[i : i + 1, :]
        lax.fori_loop(0, T // 16, norm_rows, 0, unroll=4)
        send(normed2.at[c], normed2.at[c], sibling, s_act + 2, t_act + 2)

    def wval_tile(i, _):
        left = normed2[:, :, pl.ds(pl.multiple_of(i * 512, 512), 512)].reshape(2 * T, 512)
        Gv[i] = dot(left, gv2[...].reshape(2 * T, 512), 0, 0).astype(BF16).reshape(4, 2, 2, 32, 512)
        return 0

    def wval(part):
        if part == 0:
            arrived(gv2.at[1 - c], s_act + 1)
            arrived(normed2.at[1 - c], s_act + 2)
        lax.fori_loop(2 * part, 2 * part + 2, wval_tile, 0)
        scatter_v.start_one(part)

    def normed_grad_tile(i, total):
        cols = pl.ds(pl.multiple_of(i * 512, 512), 512)
        weight = Wv[i].reshape(512, HW)
        grad = dot(gv_row[...], weight, 1, 1) * gain[:, cols]
        scaled[:, cols] = grad
        product = grad * resid[:, cols].astype(F32)
        return total + sum(product[:, 128 * k : 128 * k + 128] for k in range(4))

    def normed_grad():
        scaled[:, D:] = lax.fori_loop(0, 4, normed_grad_tile, jnp.zeros((T, 128), F32))

    def stream_rows(i, _):
        rows = pl.ds(pl.multiple_of(i * 16, 16), 16)
        inv = inverse[rows, 0:1]
        mean = jnp.sum(scaled[rows, D:], axis=-1, keepdims=True) * (1.0 / D)
        stream = resid[rows, :].astype(F32)
        result = inv * scaled[rows, :D] - stream * (inv * inv * inv * mean)
        g_patches[rows, :] = result.astype(BF16)
        return 0

    def stream_grad():
        lax.fori_loop(0, T // 16, stream_rows, 0, unroll=4)
        send(g_patches.at[:, half(1, D // 2)], gp2.at[c], sibling, s_act + 3, t_act + 3)
        gp2[c] = g_patches[:, half(0, D // 2)]

    def wout_tile(i, _):
        left = att2[:, :, pl.ds(pl.multiple_of(i * 256, 256), 256)].reshape(2 * T, 256)
        Go[i] = dot(left, gp2[...].reshape(2 * T, HW), 0, 0).astype(BF16).reshape(4, 2, 2, 16, HW)
        return 0

    def wout(part):
        if part == 0:
            arrived(att2.at[1 - c], s_act)
            arrived(gp2.at[1 - c], s_act + 3)
        lax.fori_loop(2 * part, 2 * part + 2, wout_tile, 0)
        scatter_o.start_one(part)

    def values_tile(i, _):
        cols = pl.ds(pl.multiple_of(i * 256, 256), 256)
        weight = Wv[:, :, :, :, :, cols].reshape(D, 256)
        value = dot(normed2[c], weight, 1, 0).reshape(2, 16, 8, 256)
        both = jnp.concatenate([value[0][:, None], value[1][:, None]], axis=1)
        val_out[:, cols] = both.reshape(T, 256).astype(BF16)
        return 0

    def send_values():
        lax.fori_loop(0, HW // 256, values_tile, 0)
        for k in range(1, 16):
            send(block(val_out, k), block(val_in, 0), at_row(k), s_val, t_val)
        keep_val.start()

    def take_values():
        keep_val.wait()
        all_arrived(15 * 32 * HW, s_val)

    def att_grad_tile(i, _):
        weight = Wo[i].reshape(256, D)
        g_att[:, pl.ds(pl.multiple_of(i * 256, 256), 256)] = dot(
            g_patches[...], weight, 1, 1
        ).astype(BF16)
        return 0

    def att_grad():
        lax.fori_loop(0, 4, att_grad_tile, 0)

    loaded("w_out")
    gather_o.start_z()
    cols_forward(0)
    cols_forward(1)
    cols_forward(2)
    cols_forward(3)
    send_gv()
    rows_forward(0)
    gather_o.start_two()
    take_gv()
    loaded("w_val")
    gather_v.start_z()
    gather_o.start_one()
    rows_forward(1)
    gather_v.start_two()
    rows_forward(2)
    gather_o.forward()
    gather_o.nearer()
    rows_forward(3)
    gather_v.start_one()
    gather_o.farther()
    gather_o.finish()
    residual()
    gather_v.forward()
    gather_v.nearer()
    norm()
    wval(0)
    gather_v.farther()
    wval(1)
    gather_v.finish()
    send_att()
    normed_grad()
    stream_grad()
    scatter_v.merge(0)
    scatter_v.merge(1)
    wout(0)
    wout(1)
    att_grad()
    rows_backward(0)
    rows_backward(1)
    scatter_v.start_two(1)
    scatter_v.start_two(0)
    scatter_o.merge(0)
    rows_backward(2)
    scatter_o.merge(1)
    send_values()
    scatter_o.start_two(0)
    scatter_v.end_two(1)
    rows_backward(3)
    scatter_o.start_two(1)
    scatter_v.end_two(0)
    scatter_v.start_three()
    scatter_o.end_two(0)
    take_values()
    cols_backward(0)
    scatter_o.end_two(1)
    scatter_o.start_three()
    cols_backward(1)
    scatter_v.start_four()
    cols_backward(2)
    cols_backward(3)
    scatter_v.finish()
    scatter_o.start_four()
    scatter_o.finish()
    for g, total in sent.items():
        remote(span(total), span(total), sibling, 0, g).wait_send()


def place_results(*refs):
    copies = [pltpu.make_async_copy(refs[i], refs[8 + i], refs[16].at[i]) for i in range(8)]
    for copy in copies:
        copy.start()
    for copy in copies:
        copy.wait()


def body(patches, q_rows, k_rows, v_rows, w_out, gain, w_val, q_cols, k_cols, cotangent):
    vmem = pl.BlockSpec(memory_space=pltpu.VMEM)
    outs = [(T, D), (T, HW), (T, HW), (T, HW), (T, HW), (T, HW)]
    out_shape = [jax.ShapeDtypeStruct(s, BF16) for s in outs]
    out_shape += [jax.ShapeDtypeStruct((16, D), F32), jax.ShapeDtypeStruct((32, HW), F32)]

    def reduce_buffers(rows, cols):
        h, q = cols // 2, cols // 8
        return (
            pltpu.VMEM((4, 4, 2, 2, rows, h), BF16),
            (pltpu.VMEM((2, 2, 2, rows, h), BF16), pltpu.VMEM((2, 4, 2, 2, rows, q), BF16)),
            (pltpu.VMEM((2, 2, 2, 2, rows, h), BF16), pltpu.VMEM((2, 2, 4, 2, 2, rows, q), BF16)),
            pltpu.VMEM((2, 3, 2, 2, 2, rows, q), BF16),
            pltpu.VMEM((7, 2, rows, q), BF16),
            pltpu.VMEM((2, rows, q), F32),
            pltpu.VMEM((2, 4, rows, q), F32),
        )

    ro, rv = reduce_buffers(16, D), reduce_buffers(32, HW)
    scratch = [
        pltpu.VMEM((4, 4, 2, 2, 16, D), BF16),
        pltpu.VMEM((4, 4, 2, 2, 32, HW), BF16),
        pltpu.VMEM((16, 128, 128), F32),
        pltpu.VMEM((HEADS, T, T), F32),
        pltpu.VMEM((2, T, HW), BF16),
        pltpu.VMEM((T, HW), BF16),
        pltpu.VMEM((T, HW), BF16),
        pltpu.VMEM((T, HW), BF16),
        pltpu.VMEM((2, T, HW // 2), BF16),
        pltpu.VMEM((T, D), BF16),
        pltpu.VMEM((T, 128), F32),
        pltpu.VMEM((2, T, D), BF16),
        pltpu.VMEM((T, D + 128), F32),
        pltpu.VMEM((T, HW), BF16),
        pltpu.VMEM((T, HW), BF16),
        pltpu.VMEM((2, T, D // 2), BF16),
        pltpu.VMEM((T, HW), BF16),
    ]
    for a, b in zip(ro, rv):
        scratch += [a, b]
    inputs = [(T, D), (T, HW), (T, HW), (T, HW), (16, D), (D // 128, 128), (32, HW)] + [(T, HW)] * 3
    scratch += [pltpu.VMEM(shape, BF16) for shape in inputs] + [pltpu.VMEM((1, D), F32), pltpu.VMEM((4096, 128), BF16)]
    scratch += [
        pltpu.SemaphoreType.DMA((SENDS,)),
        pltpu.SemaphoreType.DMA((RECVS,)),
        pltpu.SemaphoreType.DMA((6,)),
        pltpu.SemaphoreType.DMA((10,)),
    ]
    operands = (
        patches.reshape(T, D), q_rows.reshape(T, HW), k_rows.reshape(T, HW),
        v_rows.reshape(T, HW), w_out, gain.reshape(D // 128, 128), w_val, q_cols.reshape(T, HW),
        k_cols.reshape(T, HW), cotangent.reshape(T, HW),
    )
    operands = [pltpu.with_memory_space_constraint(a, pltpu.HBM) for a in operands]
    results = pl.pallas_call(
        kernel,
        out_shape=out_shape,
        in_specs=[pl.BlockSpec(memory_space=pltpu.HBM)] * 10,
        out_specs=[vmem] * 8,
        scratch_shapes=scratch,
        compiler_params=pltpu.CompilerParams(
            collective_id=0, has_side_effects=True, vmem_limit_bytes=46 * 2**20
        ),
        name="whole",
    )(*operands)
    anywhere = pl.BlockSpec(memory_space=pl.ANY)
    results = pl.pallas_call(
        place_results,
        out_shape=out_shape,
        in_specs=[anywhere] * 8,
        out_specs=[pl.BlockSpec(memory_space=pltpu.HBM)] * 8,
        scratch_shapes=[pltpu.SemaphoreType.DMA((8,))],
        compiler_params=pltpu.CompilerParams(vmem_limit_bytes=2**20),
        name="place",
    )(*results)
    return (
        results[0].reshape(patches.shape),
        *(results[i].reshape(q_rows.shape) for i in range(1, 4)),
        *(results[i].reshape(q_cols.shape) for i in range(4, 6)),
        results[6],
        results[7],
    )


def solution(mesh):
    rows = P(("dp", "fsdp"), "row", None, None)
    cols = P(("dp", "fsdp"), None, "row", None)
    weights = P(("fsdp", "row"), None)
    return jax.shard_map(
        body,
        mesh=mesh,
        in_specs=(rows, rows, rows, rows, weights, P(), weights, cols, cols, cols),
        out_specs=(rows, rows, rows, rows, cols, cols, weights, weights),
        check_vma=False,
    )
```
